32 devices in a mesh: grp: 2 (over x), aux: 16 (over z, y, core).
Axes of the slice: x: 2, y: 2, z: 4, core: 2. Of those that a mesh axis runs over, the one named last changes fastest.
Arguments:
- block_values: bfloat16 [2048, 128, 128], P(('grp', 'aux')), parts along dimension 0, may hold values from -0.3984375 to 0.3984375
- block_dest: int32 [2048, 1], P(('grp', 'aux')), parts along dimension 0, may hold values from 0 to 15; in each aligned block of 64 rows (0 to 63, 64 to 127, ...) at most 8 rows name the same one
- block_aux: int32 [2048], P(('grp', 'aux')), parts along dimension 0, may hold values from 0 to 15
- block_row: int32 [2048], P(('grp', 'aux')), parts along dimension 0, may hold values from 0 to 3
- block_col: int32 [2048], P(('grp', 'aux')), parts along dimension 0, may hold values from 0 to 31
- coefficients: bfloat16 [8192, 768], P('grp'), parts along dimension 0, may hold values from -0.5 to 0.5
Outputs:
- exchange_tile: float32 [1024, 512], P(('grp', 'aux')), parts along dimension 0
The draws below stay inside these ranges and needn't reach their ends.
There are 2 independent parts, one for each index of `grp`. The reference program is written for one: setup_inputs(seed, part) draws one part's arguments, and reference() takes and returns one part's arrays. A program takes and returns all parts, laid end to end along the dimension named above; each array names one. Nothing has to cross between parts.
Inputs may be any that keep to these rules, and one draw needn't show every extreme that they name: `block_dest`: of the 64 blocks of one device at most 8 go to one owner, and exactly 8 do in some aligned block of 64 rows.
All inputs are finite; a program needn't handle non-finite values.
Results may differ from the reference program's by a relative error of at most 0.0003.
Values may be sent and summed in bfloat16 or wider, within the bound.
A program may use at most 128 MiB of HBM per device.

```python
import math
import jax
import jax.numpy as jnp
import numpy as np
from jax import lax

BLK = 128
NBF = 4096
NOCC = 768
ROW_BLKS = 4
AUX_DEV = 16
NB_DEV = 64
MU = 512
BLOCKS = 1024
CAP = 8
N_AUX = 16


def plant(drawn, own_key, low, largest):
    longest = drawn.shape.index(max(drawn.shape))
    spots = []
    for shift in (0, 1):
        where = [jax.random.randint(jax.random.fold_in(own_key, axis), (), 0, length) for axis, length in enumerate(drawn.shape)]
        where[longest] = (where[longest] + shift) % drawn.shape[longest]
        spots.append(tuple(where))
    return drawn.at[spots[0]].set(low).at[spots[1]].set(largest)


def block_levels(rng, dims, shards, least, top_value):
    level, own = 1.0, jax.random.fold_in(rng, 6)
    for position, shards_of in shards:
        heights = jnp.exp(jax.random.uniform(jax.random.fold_in(own, position), (shards_of,), jnp.float32, least / len(shards), top_value / len(shards)))
        level = level * jnp.repeat(heights, dims[position] // shards_of).reshape([-1 if axis == position else 1 for axis in range(len(dims))])
    return level


def assign_block(key, own, number, rows, amount, top, reach, skew):
    order = jax.random.permutation(key, amount)
    heavy_load, common = portions_of(amount, rows * top, reach, skew, True), portions_of(amount, rows * top, reach, skew, False)
    places = jnp.arange(amount)

    def named(lengths, offset_by):
        used = int((lengths > 0).sum())
        fixed = max(1, used // 4)
        moved = fixed + (places - fixed + offset_by * (used - fixed)) % max(1, amount - fixed)
        return jnp.zeros((amount,), jnp.int32).at[order[jnp.where(places < fixed, places, moved)]].set(jnp.asarray(lengths, jnp.int32))

    lengths = jnp.where(number % 4 == 0, named(heavy_load, number // 4), named(common, number - number // 4 - 1))
    mixed = jax.random.permutation(jax.random.fold_in(own, 3), amount)
    donor, taker = mixed[0:amount // 2 * 2:2], mixed[1:amount // 2 * 2:2]
    margin = jnp.minimum(lengths[donor] - 1, reach - lengths[taker]) // 2
    margin = jnp.where((donor == order[0]) | (taker == order[0]) | (lengths[taker] == 0), 0, jnp.maximum(margin, 0))
    moved = jax.random.randint(jax.random.fold_in(own, 4), (amount // 2,), 0, 1 << 20) % (margin + 1)
    lengths = lengths.at[donor].add(-moved).at[taker].add(moved)
    items = jnp.searchsorted(jnp.cumsum(lengths), jnp.arange(rows * top), side="right").astype(jnp.int32)
    listing = items.reshape(top, rows).T
    listing = listing[jax.random.permutation(jax.random.fold_in(own, 1), rows)]
    offset_by = jax.random.randint(jax.random.fold_in(own, 2), (rows, 1), 0, top)
    return jnp.take_along_axis(listing, (jnp.arange(top)[None, :] + offset_by) % top, axis=1)


def portions_of(number_of, total, limit, skew, full):
    portions = [(1 << 20) // math.isqrt(standing ** skew) + 1 for standing in range(1, number_of + 1)]
    largest = limit if full else min(limit, max(-(-total // number_of), total * portions[0] // sum(portions)))
    least = 1 if total - largest >= number_of - 1 else 0
    given, surplus = [largest] + [least] * (number_of - 1), total - largest - least * (number_of - 1)
    while surplus > 0:
        candidates = [i for i in range(1, number_of) if given[i] < largest] or [i for i in range(1, number_of) if given[i] < limit]
        mass, left = sum([portions[i] for i in candidates]), surplus
        for i in candidates:
            extra = min(limit - given[i], max(1, left * portions[i] // mass), surplus)
            given[i] = given[i] + extra
            surplus = surplus - extra
    return np.array(given)


def scatter_about(stream_key, dims, width, reach, cuts=(), held_as=jnp.bfloat16):
    values = width * jax.random.normal(stream_key, dims, jnp.float32)
    if cuts:
        values = values * block_levels(stream_key, dims, cuts, -0.22, 0.18)
    return jnp.clip(values, -reach, reach).astype(held_as)


def setup_inputs(seed: int = 0, part: int = 0) -> dict:
    streams_of = jax.random.split(jax.random.key(seed), 7)
    own_keys = jax.random.split(jax.random.fold_in(streams_of[6], part), 7)
    block_values = scatter_about(own_keys[0], (BLOCKS, BLK, BLK), 0.0625, 0.3984375, ((0, 16),))
    block_dest_keys = jax.random.split(jax.random.fold_in(own_keys[1], 1), BLOCKS // NB_DEV)
    block_dest_turns = jax.random.permutation(jax.random.fold_in(own_keys[1], 3), BLOCKS // NB_DEV)
    block_dest = jax.vmap(lambda own, number: assign_block(jax.random.fold_in(own_keys[1], 2), own, number, NB_DEV, N_AUX, 1, CAP, 2))(block_dest_keys, block_dest_turns).reshape((BLOCKS, 1))
    block_aux = plant(jax.random.randint(own_keys[2], (BLOCKS,), 0, AUX_DEV), jax.random.fold_in(own_keys[2], 1), 0, AUX_DEV - 1).astype(jnp.int32)
    block_row = plant(jax.random.randint(own_keys[3], (BLOCKS,), 0, ROW_BLKS), jax.random.fold_in(own_keys[3], 1), 0, ROW_BLKS - 1).astype(jnp.int32)
    block_col = plant(jax.random.randint(own_keys[4], (BLOCKS,), 0, NBF // BLK), jax.random.fold_in(own_keys[4], 1), 0, (NBF // BLK) - 1).astype(jnp.int32)
    coefficients = scatter_about(own_keys[5], (NBF, NOCC), BLK ** -0.5, 0.5)
    return dict(block_values=block_values, block_dest=block_dest, block_aux=block_aux, block_row=block_row, block_col=block_col, coefficients=coefficients)


def reference(block_values, block_dest, block_aux, block_row, block_col, coefficients):
    dest = block_dest[:, 0].astype(jnp.int32)
    window = 2 * NB_DEV
    order = jnp.argsort(dest, stable=True).astype(jnp.int32)
    owners = jnp.arange(N_AUX, dtype=jnp.int32)
    counts = jnp.sum((dest[None, :] == owners[:, None]).astype(jnp.int32), axis=1)
    starts = (jnp.cumsum(counts) - counts).astype(jnp.int32)
    values_p = jnp.concatenate([block_values[order], jnp.zeros((window, BLK, BLK), block_values.dtype)], axis=0)
    dest_p = jnp.concatenate([dest[order], jnp.full((window,), -1, jnp.int32)], axis=0)
    aux_p = jnp.concatenate([block_aux[order], jnp.zeros((window,), jnp.int32)], axis=0)
    row_p = jnp.concatenate([block_row[order], jnp.zeros((window,), jnp.int32)], axis=0)
    col_p = jnp.concatenate([block_col[order], jnp.zeros((window,), jnp.int32)], axis=0)
    col_tiles = coefficients.reshape(NBF // BLK, BLK, NOCC)

    def per_owner(total_tile, owner):
        picks = (starts[owner] + jnp.arange(window, dtype=jnp.int32)).astype(jnp.int32)
        values = values_p[picks].astype(jnp.float32)
        live = (dest_p[picks] == owner).astype(jnp.float32)
        tiles = col_tiles[col_p[picks]].astype(jnp.float32)
        part = jnp.einsum('smn,sni->smi', values, tiles) * live[:, None, None]
        half = jnp.zeros((ROW_BLKS, BLK, AUX_DEV, NOCC), jnp.float32)
        half = half.at[row_p[picks], :, aux_p[picks]].add(part)
        rounded = half.astype(jnp.bfloat16).reshape(MU, AUX_DEV * NOCC)
        product = jnp.dot(rounded, rounded.T, preferred_element_type=jnp.float32)
        return total_tile + product, None

    result, unused = lax.scan(per_owner, jnp.zeros((MU, MU), jnp.float32), owners)
    return result / NOCC
```

```python
import functools

import jax
import jax.numpy as jnp
from jax import lax
from jax.experimental import pallas as pl
from jax.experimental.pallas import tpu as pltpu
from jax.sharding import PartitionSpec as P

ROW_BLKS = 4
AUX_DEV = 16
KEYS = ROW_BLKS * AUX_DEV
MU = 512
MESH = pl.DeviceIdType.MESH
VMEM = pl.BlockSpec(memory_space=pltpu.VMEM)
SMEM = pl.BlockSpec(memory_space=pltpu.SMEM)
ANY = pl.BlockSpec(memory_space=pl.ANY)


def greet(others):
    barrier = pltpu.get_barrier_semaphore()
    for other in others:
        pl.semaphore_signal(barrier, inc=1, device_id={"aux": other}, device_id_type=MESH)
    pl.semaphore_wait(barrier, len(others))


def exchange_kernel(
    n, slots, idx_ref, vals_ref, code_ref, out_ref, code_out,
    packed, send_sem, recv_sem, csend_sem, crecv_sem, own_sem,
):
    me = lax.axis_index("aux")
    greet([lax.rem(me + d, n) for d in range(1, n)])

    def copies(d):
        peer = lax.rem(me + d, n)
        values = pltpu.make_async_remote_copy(
            src_ref=packed.at[peer],
            dst_ref=out_ref.at[me],
            send_sem=send_sem.at[d],
            recv_sem=recv_sem.at[d],
            device_id={"aux": peer},
            device_id_type=MESH,
        )
        codes = pltpu.make_async_remote_copy(
            src_ref=code_ref.at[peer],
            dst_ref=code_out.at[me],
            send_sem=csend_sem.at[d],
            recv_sem=crecv_sem.at[d],
            device_id={"aux": peer},
            device_id_type=MESH,
        )
        return values, codes

    def pack(peer):
        for k in range(slots):
            packed[peer, k] = vals_ref[idx_ref[peer * slots + k]]

    def send(d, carry):
        pack(lax.rem(me + d, n))
        values, codes = copies(d)
        codes.start()
        values.start()
        return carry

    lax.fori_loop(1, n, send, 0)
    pack(me)
    own_values = pltpu.make_async_copy(packed.at[me], out_ref.at[me], own_sem.at[0])
    own_codes = pltpu.make_async_copy(code_ref.at[me], code_out.at[me], own_sem.at[1])
    own_values.start()
    own_codes.start()
    own_values.wait()
    own_codes.wait()

    def finish(d, carry):
        values, codes = copies(d)
        codes.wait()
        values.wait()
        return carry

    lax.fori_loop(1, n, finish, 0)


def exchange(n, slots, idx, vals, codes):
    side = vals.shape[1]
    return pl.pallas_call(
        functools.partial(exchange_kernel, n, slots),
        out_shape=(
            jax.ShapeDtypeStruct((n, slots, side, side), vals.dtype),
            jax.ShapeDtypeStruct(codes.shape, codes.dtype),
        ),
        in_specs=[SMEM, VMEM, VMEM],
        out_specs=(ANY, ANY),
        scratch_shapes=[
            pltpu.VMEM((n, slots, side, side), vals.dtype),
            pltpu.SemaphoreType.DMA((n,)),
            pltpu.SemaphoreType.DMA((n,)),
            pltpu.SemaphoreType.DMA((n,)),
            pltpu.SemaphoreType.DMA((n,)),
            pltpu.SemaphoreType.DMA((2,)),
        ],
        compiler_params=pltpu.CompilerParams(
            collective_id=0, has_side_effects=True, vmem_limit_bytes=24 * 2**20
        ),
    )(idx, vals, codes)


def tile_kernel(n, slots, code_ref, vals_ref, coef_ref, out_ref, acc):
    side = vals_ref.shape[1]

    def clear(a, carry):
        acc[a] = jnp.zeros(acc.shape[1:], jnp.float32)
        return carry

    lax.fori_loop(0, AUX_DEV, clear, 0)

    def add(step, carry):
        for k in range(slots):
            s = step * slots + k
            code = code_ref[s]
            key = jnp.where(code >= 0, code % KEYS, KEYS)
            col = jnp.where(code >= 0, code // KEYS, 0)
            part = jnp.dot(vals_ref[s], coef_ref[col], preferred_element_type=jnp.float32)
            rows = pl.ds(pl.multiple_of(key % ROW_BLKS * side, side), side)
            acc[key // ROW_BLKS, rows, :] += part
        return carry

    lax.fori_loop(0, n, add, 0)
    out_ref[...] = jnp.zeros_like(out_ref)

    def square(a, carry):
        half = acc[a].astype(jnp.bfloat16)
        out_ref[...] += lax.dot_general(
            half, half, (((1,), (1,)), ((), ())), preferred_element_type=jnp.float32
        )
        return carry

    lax.fori_loop(0, AUX_DEV, square, 0)


def tile(n, slots, codes, vals, coef):
    nocc = coef.shape[2]
    return pl.pallas_call(
        functools.partial(tile_kernel, n, slots),
        out_shape=jax.ShapeDtypeStruct((MU, MU), jnp.float32),
        in_specs=[SMEM, VMEM, VMEM],
        out_specs=VMEM,
        scratch_shapes=[pltpu.VMEM((AUX_DEV + 1, MU, nocc), jnp.float32)],
        compiler_params=pltpu.CompilerParams(vmem_limit_bytes=56 * 2**20),
    )(codes, vals, coef)


def reduce_kernel(n, scale, k_ref, out_ref, got1, sum1, got2, sum2, got3, send_sem, recv_sem):
    me = lax.axis_index("aux")
    far = n // 4
    c, y, z = me % 2, me // 2 % 2, me // 4
    pair, side = me + 1 - 2 * c, me + 2 - 4 * y
    greet([pair, side] + [lax.rem(me + 4 * d, n) for d in range(1, far)])

    def copy(src, dst, sem, other):
        return pltpu.make_async_remote_copy(
            src_ref=src,
            dst_ref=dst,
            send_sem=send_sem.at[sem],
            recv_sem=recv_sem.at[sem],
            device_id={"aux": other},
            device_id_type=MESH,
        )

    first = copy(k_ref.at[:, :, 1 - c], got1, 0, pair)
    first.start()
    first.wait()
    sum1[...] = k_ref[:, :, c] + got1[...]
    second = copy(sum1.at[:, 1 - y], got2, 1, side)
    second.start()
    second.wait()
    sum2[...] = sum1[:, y] + got2[...]
    third = [
        copy(sum2.at[lax.rem(z + d, far)], got3.at[d - 1], 1 + d, lax.rem(me + 4 * d, n))
        for d in range(1, far)
    ]
    for one in third:
        one.start()
    total = sum2[z]
    for d, one in enumerate(third):
        one.wait()
        total = total + got3[d]
    out_ref[...] = total * scale


def reduce_tile(n, scale, whole):
    far, rows = n // 4, MU // n
    f32 = jnp.float32
    return pl.pallas_call(
        functools.partial(reduce_kernel, n, scale),
        out_shape=jax.ShapeDtypeStruct((rows, MU), f32),
        in_specs=[VMEM],
        out_specs=VMEM,
        scratch_shapes=[
            pltpu.VMEM((far, 2, rows, MU), f32),
            pltpu.VMEM((far, 2, rows, MU), f32),
            pltpu.VMEM((far, rows, MU), f32),
            pltpu.VMEM((far, rows, MU), f32),
            pltpu.VMEM((far - 1, rows, MU), f32),
            pltpu.SemaphoreType.DMA((far + 1,)),
            pltpu.SemaphoreType.DMA((far + 1,)),
        ],
        compiler_params=pltpu.CompilerParams(
            collective_id=1, has_side_effects=True, vmem_limit_bytes=16 * 2**20
        ),
    )(whole.reshape(far, 2, 2, rows, MU))


def body(block_values, block_dest, block_aux, block_row, block_col, coefficients):
    n = lax.axis_size("aux")
    count, side = block_values.shape[:2]
    nocc = coefficients.shape[1]
    slots = 2 * count // n
    dest = block_dest[:, 0]
    place = jnp.arange(count, dtype=jnp.int32)
    earlier = (dest[:, None] == dest[None, :]) & (place[:, None] > place[None, :])
    target = dest * slots + jnp.sum(earlier.astype(jnp.int32), axis=1)
    hit = target[None, :] == jnp.arange(n * slots, dtype=jnp.int32)[:, None]
    idx = jnp.sum(jnp.where(hit, place[None, :], 0), axis=1)
    code = block_col * KEYS + block_aux * ROW_BLKS + block_row
    sent = jnp.sum(jnp.where(hit, code[None, :] + 1, 0), axis=1) - 1
    sent = jnp.pad(sent.reshape(n, 1, slots), ((0, 0), (0, 7), (0, 128 - slots)))
    values, codes = exchange(n, slots, idx, block_values, sent)
    whole = tile(
        n,
        slots,
        codes[:, 0, :slots].reshape(n * slots),
        values.reshape(n * slots, side, side),
        coefficients.reshape(-1, side, nocc),
    )
    return reduce_tile(n, 1.0 / nocc, whole)


def solution(mesh):
    placed = (
        P(("grp", "aux"), None, None),
        P(("grp", "aux"), None),
        P(("grp", "aux")),
        P(("grp", "aux")),
        P(("grp", "aux")),
        P("grp", None),
    )
    return jax.shard_map(
        body, mesh=mesh, in_specs=placed, out_specs=P(("grp", "aux"), None), check_vma=False
    )
```

```python
import functools

import jax
import jax.numpy as jnp
from jax import lax
from jax.experimental import pallas as pl
from jax.experimental.pallas import tpu as pltpu
from jax.sharding import PartitionSpec as P

ROW_BLKS = 4
AUX_DEV = 16
KEYS = ROW_BLKS * AUX_DEV
MU = 512
MESH = pl.DeviceIdType.MESH
VMEM = pl.BlockSpec(memory_space=pltpu.VMEM)
SMEM = pl.BlockSpec(memory_space=pltpu.SMEM)
ANY = pl.BlockSpec(memory_space=pl.ANY)


def paired(me, d, n):
    peer, bit = 0, 1
    while bit < n:
        mine, other = me // bit % 2, d // bit % 2
        peer = peer + bit * (mine + other - 2 * mine * other)
        bit *= 2
    return peer


def greet(others):
    barrier = pltpu.get_barrier_semaphore()
    for other in others:
        pl.semaphore_signal(barrier, inc=1, device_id={"aux": other}, device_id_type=MESH)
    pl.semaphore_wait(barrier, len(others))


def exchange_kernel(
    n, slots, idx_ref, vals_ref, code_ref, out_ref, code_out,
    packed, send_sem, recv_sem, csend_sem, crecv_sem, own_sem,
):
    me = lax.axis_index("aux")
    greet([paired(me, d, n) for d in range(1, n)])

    def copies(d):
        peer = paired(me, d, n)
        values = pltpu.make_async_remote_copy(
            src_ref=packed.at[peer],
            dst_ref=out_ref.at[me],
            send_sem=send_sem.at[d],
            recv_sem=recv_sem.at[d],
            device_id={"aux": peer},
            device_id_type=MESH,
        )
        codes = pltpu.make_async_remote_copy(
            src_ref=code_ref.at[peer],
            dst_ref=code_out.at[me],
            send_sem=csend_sem.at[d],
            recv_sem=crecv_sem.at[d],
            device_id={"aux": peer},
            device_id_type=MESH,
        )
        return values, codes

    def pack(peer):
        for k in range(slots):
            packed[peer, k] = vals_ref[idx_ref[peer * slots + k]]

    def send(step, carry):
        d = n - step
        pack(paired(me, d, n))
        values, codes = copies(d)
        codes.start()
        values.start()
        return carry

    lax.fori_loop(1, n, send, 0)
    pack(me)
    own_values = pltpu.make_async_copy(packed.at[me], out_ref.at[me], own_sem.at[0])
    own_codes = pltpu.make_async_copy(code_ref.at[me], code_out.at[me], own_sem.at[1])
    own_values.start()
    own_codes.start()
    own_values.wait()
    own_codes.wait()

    def finish(d, carry):
        values, codes = copies(d)
        codes.wait()
        values.wait()
        return carry

    lax.fori_loop(1, n, finish, 0)


def exchange(n, slots, idx, vals, codes):
    side = vals.shape[1]
    return pl.pallas_call(
        functools.partial(exchange_kernel, n, slots),
        out_shape=(
            jax.ShapeDtypeStruct((n, slots, side, side), vals.dtype),
            jax.ShapeDtypeStruct(codes.shape, codes.dtype),
        ),
        in_specs=[SMEM, VMEM, VMEM],
        out_specs=(ANY, ANY),
        scratch_shapes=[
            pltpu.VMEM((n, slots, side, side), vals.dtype),
            pltpu.SemaphoreType.DMA((n,)),
            pltpu.SemaphoreType.DMA((n,)),
            pltpu.SemaphoreType.DMA((n,)),
            pltpu.SemaphoreType.DMA((n,)),
            pltpu.SemaphoreType.DMA((2,)),
        ],
        compiler_params=pltpu.CompilerParams(
            collective_id=0, has_side_effects=True, vmem_limit_bytes=24 * 2**20
        ),
    )(idx, vals, codes)


def tile_kernel(n, slots, code_ref, vals_ref, coef_ref, out_ref, acc, seen):
    side = vals_ref.shape[1]
    mid = MU // 2

    def reset(key, carry):
        seen[key] = 0
        return carry

    lax.fori_loop(0, KEYS + 1, reset, 0)

    def add(step, carry):
        for k in range(slots):
            s = step * slots + k
            code = code_ref[s]
            key = jnp.where(code >= 0, code % KEYS, KEYS)
            col = jnp.where(code >= 0, code // KEYS, 0)
            part = jnp.dot(vals_ref[s], coef_ref[col], preferred_element_type=jnp.float32)
            rows = pl.ds(pl.multiple_of(key % ROW_BLKS * side, side), side)
            before = jnp.where(seen[key] == 1, acc[key // ROW_BLKS, rows, :], 0.0)
            acc[key // ROW_BLKS, rows, :] = before + part
            seen[key] = 1
        return carry

    lax.fori_loop(0, n, add, 0)
    out_ref[...] = jnp.zeros_like(out_ref)

    def against(left, right):
        return lax.dot_general(
            left, right, (((1,), (1,)), ((), ())), preferred_element_type=jnp.float32
        )

    def rounded(a):
        return jnp.concatenate(
            [
                jnp.where(
                    seen[a * ROW_BLKS + r] == 1, acc[a, r * side : (r + 1) * side, :], 0.0
                ).astype(jnp.bfloat16)
                for r in range(ROW_BLKS)
            ],
            axis=0,
        )

    def square(step, carry):
        h, g = rounded(2 * step), rounded(2 * step + 1)
        out_ref[:mid, :] += against(h[:mid], h) + against(g[:mid], g)
        out_ref[mid:, mid:] += against(h[mid:], h[mid:]) + against(g[mid:], g[mid:])
        return carry

    lax.fori_loop(0, AUX_DEV // 2, square, 0)
    out_ref[mid:, :mid] = out_ref[:mid, mid:].T


def tile(n, slots, codes, vals, coef):
    nocc = coef.shape[2]
    return pl.pallas_call(
        functools.partial(tile_kernel, n, slots),
        out_shape=jax.ShapeDtypeStruct((MU, MU), jnp.float32),
        in_specs=[SMEM, VMEM, VMEM],
        out_specs=VMEM,
        scratch_shapes=[
            pltpu.VMEM((AUX_DEV + 1, MU, nocc), jnp.float32),
            pltpu.SMEM((KEYS + 1,), jnp.int32),
        ],
        compiler_params=pltpu.CompilerParams(vmem_limit_bytes=56 * 2**20),
    )(codes, vals, coef)


def reduce_kernel(n, scale, k_ref, out_ref, got1, sum1, got2, sum2, got3, send_sem, recv_sem):
    me = lax.axis_index("aux")
    far = n // 4
    c, y, z = me % 2, me // 2 % 2, me // 4
    pair, side = me + 1 - 2 * c, me + 2 - 4 * y
    order = list(range(far - 1, -1, -1))
    chunk = [paired(z, t, far) for t in range(far)]
    greet([pair, side] + [me + 4 * (chunk[t] - z) for t in range(1, far)])

    def copy(src, dst, sem, other):
        return pltpu.make_async_remote_copy(
            src_ref=src,
            dst_ref=dst,
            send_sem=send_sem.at[sem],
            recv_sem=recv_sem.at[sem],
            device_id={"aux": other},
            device_id_type=MESH,
        )

    def across(t, half, sem):
        spot = chunk[t]
        return copy(k_ref.at[spot, half, 1 - c], got1.at[spot, half], sem, pair)

    give = [across(t, 1 - y, t) for t in range(far)]
    keep = [across(t, y, far + t) for t in range(far)]
    beside = [copy(sum1.at[t], got2.at[t], 2 * far + t, side) for t in range(far)]
    along = [
        copy(sum2.at[t], got3.at[t], 3 * far + t, me + 4 * (chunk[t] - z)) for t in range(far)
    ]
    for t in order:
        give[t].start()
    for t in order:
        keep[t].start()
    for t in order:
        give[t].wait()
        sum1[t] = k_ref[chunk[t], 1 - y, c] + got1[chunk[t], 1 - y]
        beside[t].start()
    for t in order:
        keep[t].wait()
        mine = k_ref[chunk[t], y, c] + got1[chunk[t], y]
        beside[t].wait()
        sum2[t] = mine + got2[t]
        if t:
            along[t].start()
    total = sum2[0]
    for t in order[:-1]:
        along[t].wait()
        total = total + got3[t]
    out_ref[...] = total * scale


def reduce_tile(n, scale, whole):
    far, rows = n // 4, MU // n
    f32 = jnp.float32
    return pl.pallas_call(
        functools.partial(reduce_kernel, n, scale),
        out_shape=jax.ShapeDtypeStruct((rows, MU), f32),
        in_specs=[VMEM],
        out_specs=VMEM,
        scratch_shapes=[
            pltpu.VMEM((far, 2, rows, MU), f32),
            pltpu.VMEM((far, rows, MU), f32),
            pltpu.VMEM((far, rows, MU), f32),
            pltpu.VMEM((far, rows, MU), f32),
            pltpu.VMEM((far, rows, MU), f32),
            pltpu.SemaphoreType.DMA((4 * far,)),
            pltpu.SemaphoreType.DMA((4 * far,)),
        ],
        compiler_params=pltpu.CompilerParams(
            collective_id=1, has_side_effects=True, vmem_limit_bytes=16 * 2**20
        ),
    )(whole.reshape(far, 2, 2, rows, MU))


def body(block_values, block_dest, block_aux, block_row, block_col, coefficients):
    n = lax.axis_size("aux")
    count, side = block_values.shape[:2]
    nocc = coefficients.shape[1]
    slots = 2 * count // n
    dest = block_dest[:, 0]
    place = jnp.arange(count, dtype=jnp.int32)
    earlier = (dest[:, None] == dest[None, :]) & (place[:, None] > place[None, :])
    target = dest * slots + jnp.sum(earlier.astype(jnp.int32), axis=1)
    hit = target[None, :] == jnp.arange(n * slots, dtype=jnp.int32)[:, None]
    idx = jnp.sum(jnp.where(hit, place[None, :], 0), axis=1)
    code = block_col * KEYS + block_aux * ROW_BLKS + block_row
    sent = jnp.sum(jnp.where(hit, code[None, :] + 1, 0), axis=1) - 1
    sent = jnp.pad(sent.reshape(n, 1, slots), ((0, 0), (0, 7), (0, 128 - slots)))
    values, codes = exchange(n, slots, idx, block_values, sent)
    whole = tile(
        n,
        slots,
        codes[:, 0, :slots].reshape(n * slots),
        values.reshape(n * slots, side, side),
        coefficients.reshape(-1, side, nocc),
    )
    return reduce_tile(n, 1.0 / nocc, whole)


def solution(mesh):
    placed = (
        P(("grp", "aux"), None, None),
        P(("grp", "aux"), None),
        P(("grp", "aux")),
        P(("grp", "aux")),
        P(("grp", "aux")),
        P("grp", None),
    )
    return jax.shard_map(
        body, mesh=mesh, in_specs=placed, out_specs=P(("grp", "aux"), None), check_vma=False
    )
```

```python
import functools

import jax
import jax.numpy as jnp
from jax import lax
from jax.experimental import pallas as pl
from jax.experimental.pallas import tpu as pltpu
from jax.sharding import PartitionSpec as P

ROW_BLKS = 4
AUX_DEV = 16
KEYS = ROW_BLKS * AUX_DEV
MU = 512
MESH = pl.DeviceIdType.MESH
VMEM = pl.BlockSpec(memory_space=pltpu.VMEM)
SMEM = pl.BlockSpec(memory_space=pltpu.SMEM)
ANY = pl.BlockSpec(memory_space=pl.ANY)


def paired(me, d, n):
    peer, bit = 0, 1
    while bit < n:
        mine, other = me // bit % 2, d // bit % 2
        peer = peer + bit * (mine + other - 2 * mine * other)
        bit *= 2
    return peer


def greet(others):
    barrier = pltpu.get_barrier_semaphore()
    for other in others:
        pl.semaphore_signal(barrier, inc=1, device_id={"aux": other}, device_id_type=MESH)
    pl.semaphore_wait(barrier, len(others))


def exchange_kernel(
    n, slots, idx_ref, vals_ref, code_ref, out_ref, code_out,
    blocks, packed, send_sem, recv_sem, csend_sem, crecv_sem, own_sem,
):
    me = lax.axis_index("aux")
    load = pltpu.make_async_copy(vals_ref, blocks, own_sem.at[2])
    load.start()
    greet([paired(me, d, n) for d in range(1, n)])

    def copies(d):
        peer = paired(me, d, n)
        values = pltpu.make_async_remote_copy(
            src_ref=packed.at[peer],
            dst_ref=out_ref.at[me],
            send_sem=send_sem.at[d],
            recv_sem=recv_sem.at[d],
            device_id={"aux": peer},
            device_id_type=MESH,
        )
        codes = pltpu.make_async_remote_copy(
            src_ref=code_ref.at[peer],
            dst_ref=code_out.at[me],
            send_sem=csend_sem.at[d],
            recv_sem=crecv_sem.at[d],
            device_id={"aux": peer},
            device_id_type=MESH,
        )
        return values, codes

    def pack(peer):
        for k in range(slots):
            packed[peer, k] = blocks[idx_ref[peer * slots + k]]

    half = n // 2
    lead = half // 4 * (me % 4)

    def send(step, carry):
        at = step - 1
        inner = half - 1 - (at - lead)
        outer = n - 1 - jnp.where(at < lead, at, at - (half - 1))
        d = jnp.where((at >= lead) & (at < lead + half - 1), inner, outer)
        pack(paired(me, d, n))
        values, codes = copies(d)
        codes.start()
        values.start()
        return carry

    load.wait()
    lax.fori_loop(1, n, send, 0)
    pack(me)
    own_values = pltpu.make_async_copy(packed.at[me], out_ref.at[me], own_sem.at[0])
    own_codes = pltpu.make_async_copy(code_ref.at[me], code_out.at[me], own_sem.at[1])
    own_values.start()
    own_codes.start()
    own_values.wait()
    own_codes.wait()

    def finish(d, carry):
        values, codes = copies(d)
        codes.wait()
        values.wait()
        return carry

    lax.fori_loop(1, n, finish, 0)


def exchange(n, slots, idx, vals, codes):
    side = vals.shape[1]
    return pl.pallas_call(
        functools.partial(exchange_kernel, n, slots),
        out_shape=(
            jax.ShapeDtypeStruct((n, slots, side, side), vals.dtype),
            jax.ShapeDtypeStruct(codes.shape, codes.dtype),
        ),
        in_specs=[SMEM, ANY, VMEM],
        out_specs=(ANY, ANY),
        scratch_shapes=[
            pltpu.VMEM(vals.shape, vals.dtype),
            pltpu.VMEM((n, slots, side, side), vals.dtype),
            pltpu.SemaphoreType.DMA((n,)),
            pltpu.SemaphoreType.DMA((n,)),
            pltpu.SemaphoreType.DMA((n,)),
            pltpu.SemaphoreType.DMA((n,)),
            pltpu.SemaphoreType.DMA((3,)),
        ],
        compiler_params=pltpu.CompilerParams(
            collective_id=0, has_side_effects=True, vmem_limit_bytes=8 * 2**20
        ),
    )(idx, vals, codes)


def tile_kernel(n, slots, code_ref, vals_ref, coef_ref, out_ref, acc, seen):
    side = vals_ref.shape[1]
    mid = MU // 2

    def reset(key, carry):
        seen[key] = 0
        return carry

    lax.fori_loop(0, KEYS + 1, reset, 0)

    def add(step, carry):
        for k in range(slots):
            s = step * slots + k
            code = code_ref[s]
            key = jnp.where(code >= 0, code % KEYS, KEYS)
            col = jnp.where(code >= 0, code // KEYS, 0)
            part = jnp.dot(vals_ref[s], coef_ref[col], preferred_element_type=jnp.float32)
            rows = pl.ds(pl.multiple_of(key % ROW_BLKS * side, side), side)
            before = jnp.where(seen[key] == 1, acc[key // ROW_BLKS, rows, :], 0.0)
            acc[key // ROW_BLKS, rows, :] = before + part
            seen[key] = 1
        return carry

    lax.fori_loop(0, n, add, 0)
    out_ref[...] = jnp.zeros_like(out_ref)

    def against(left, right):
        return lax.dot_general(
            left, right, (((1,), (1,)), ((), ())), preferred_element_type=jnp.float32
        )

    def rounded(a):
        return jnp.concatenate(
            [
                jnp.where(
                    seen[a * ROW_BLKS + r] == 1, acc[a, r * side : (r + 1) * side, :], 0.0
                ).astype(jnp.bfloat16)
                for r in range(ROW_BLKS)
            ],
            axis=0,
        )

    def square(step, carry):
        h, g = rounded(2 * step), rounded(2 * step + 1)
        out_ref[:mid, :] += against(h[:mid], h) + against(g[:mid], g)
        out_ref[mid:, mid:] += against(h[mid:], h[mid:]) + against(g[mid:], g[mid:])
        return carry

    lax.fori_loop(0, AUX_DEV // 2, square, 0)
    out_ref[mid:, :mid] = out_ref[:mid, mid:].T


def tile(n, slots, codes, vals, coef):
    nocc = coef.shape[2]
    return pl.pallas_call(
        functools.partial(tile_kernel, n, slots),
        out_shape=jax.ShapeDtypeStruct((MU, MU), jnp.float32),
        in_specs=[SMEM, VMEM, VMEM],
        out_specs=VMEM,
        scratch_shapes=[
            pltpu.VMEM((AUX_DEV + 1, MU, nocc), jnp.float32),
            pltpu.SMEM((KEYS + 1,), jnp.int32),
        ],
        compiler_params=pltpu.CompilerParams(vmem_limit_bytes=42 * 2**20),
    )(codes, vals, coef)


def reduce_kernel(n, scale, k_ref, out_ref, got1, sum1, got2, sum2, got3, send_sem, recv_sem):
    me = lax.axis_index("aux")
    far = n // 4
    c, y, z = me % 2, me // 2 % 2, me // 4
    pair, side = me + 1 - 2 * c, me + 2 - 4 * y
    order = list(range(far - 1, -1, -1))
    chunk = [paired(z, t, far) for t in range(far)]
    greet([pair, side] + [me + 4 * (chunk[t] - z) for t in range(1, far)])

    def copy(src, dst, sem, other):
        return pltpu.make_async_remote_copy(
            src_ref=src,
            dst_ref=dst,
            send_sem=send_sem.at[sem],
            recv_sem=recv_sem.at[sem],
            device_id={"aux": other},
            device_id_type=MESH,
        )

    def across(t, half, sem):
        spot = chunk[t]
        return copy(k_ref.at[spot, half, 1 - c], got1.at[spot, half], sem, pair)

    give = [across(t, 1 - y, t) for t in range(far)]
    keep = [across(t, y, far + t) for t in range(far)]
    beside = [copy(sum1.at[t], got2.at[t], 2 * far + t, side) for t in range(far)]
    along = [
        copy(sum2.at[t], got3.at[t], 3 * far + t, me + 4 * (chunk[t] - z)) for t in range(far)
    ]
    for t in order:
        give[t].start()
    for t in order:
        keep[t].start()
    for t in order:
        give[t].wait()
        sum1[t] = k_ref[chunk[t], 1 - y, c] + got1[chunk[t], 1 - y]
        beside[t].start()
    for t in order:
        keep[t].wait()
        mine = k_ref[chunk[t], y, c] + got1[chunk[t], y]
        beside[t].wait()
        sum2[t] = mine + got2[t]
        if t:
            along[t].start()
    total = sum2[0]
    for t in order[:-1]:
        along[t].wait()
        total = total + got3[t]
    out_ref[...] = total * scale


def reduce_tile(n, scale, whole):
    far, rows = n // 4, MU // n
    f32 = jnp.float32
    return pl.pallas_call(
        functools.partial(reduce_kernel, n, scale),
        out_shape=jax.ShapeDtypeStruct((rows, MU), f32),
        in_specs=[VMEM],
        out_specs=VMEM,
        scratch_shapes=[
            pltpu.VMEM((far, 2, rows, MU), f32),
            pltpu.VMEM((far, rows, MU), f32),
            pltpu.VMEM((far, rows, MU), f32),
            pltpu.VMEM((far, rows, MU), f32),
            pltpu.VMEM((far, rows, MU), f32),
            pltpu.SemaphoreType.DMA((4 * far,)),
            pltpu.SemaphoreType.DMA((4 * far,)),
        ],
        compiler_params=pltpu.CompilerParams(
            collective_id=1, has_side_effects=True, vmem_limit_bytes=6 * 2**20
        ),
    )(whole.reshape(far, 2, 2, rows, MU))


def body(block_values, block_dest, block_aux, block_row, block_col, coefficients):
    n = lax.axis_size("aux")
    count, side = block_values.shape[:2]
    nocc = coefficients.shape[1]
    slots = 2 * count // n
    dest = block_dest[:, 0]
    place = jnp.arange(count, dtype=jnp.int32)
    earlier = (dest[:, None] == dest[None, :]) & (place[:, None] > place[None, :])
    target = dest * slots + jnp.sum(earlier.astype(jnp.int32), axis=1)
    hit = target[None, :] == jnp.arange(n * slots, dtype=jnp.int32)[:, None]
    idx = jnp.sum(jnp.where(hit, place[None, :], 0), axis=1)
    code = block_col * KEYS + block_aux * ROW_BLKS + block_row
    sent = jnp.sum(jnp.where(hit, code[None, :] + 1, 0), axis=1) - 1
    sent = jnp.pad(sent.reshape(n, 1, slots), ((0, 0), (0, 7), (0, 128 - slots)))
    values, codes = exchange(n, slots, idx, block_values, sent)
    whole = tile(
        n,
        slots,
        codes[:, 0, :slots].reshape(n * slots),
        values.reshape(n * slots, side, side),
        coefficients.reshape(-1, side, nocc),
    )
    return reduce_tile(n, 1.0 / nocc, whole)


def solution(mesh):
    placed = (
        P(("grp", "aux"), None, None),
        P(("grp", "aux"), None),
        P(("grp", "aux")),
        P(("grp", "aux")),
        P(("grp", "aux")),
        P("grp", None),
    )
    return jax.shard_map(
        body, mesh=mesh, in_specs=placed, out_specs=P(("grp", "aux"), None), check_vma=False
    )
```

```python
import functools

import jax
import jax.numpy as jnp
from jax import lax
from jax.experimental import pallas as pl
from jax.experimental.pallas import tpu as pltpu
from jax.sharding import PartitionSpec as P

ROW_BLKS = 4
AUX_DEV = 16
KEYS = ROW_BLKS * AUX_DEV
MU = 512
MESH = pl.DeviceIdType.MESH
VMEM = pl.BlockSpec(memory_space=pltpu.VMEM)
SMEM = pl.BlockSpec(memory_space=pltpu.SMEM)
ANY = pl.BlockSpec(memory_space=pl.ANY)


def paired(me, d, n):
    peer, bit = 0, 1
    while bit < n:
        mine, other = me // bit % 2, d // bit % 2
        peer = peer + bit * (mine + other - 2 * mine * other)
        bit *= 2
    return peer


def greet(others):
    barrier = pltpu.get_barrier_semaphore()
    for other in others:
        pl.semaphore_signal(barrier, inc=1, device_id={"aux": other}, device_id_type=MESH)
    pl.semaphore_wait(barrier, len(others))


def spread(n, slots):
    chips = n // 2
    full = [q for q in range(chips) if (q // 2 + q) % 2 == 0]
    rest = [q for q in range(chips) if (q // 2 + q) % 2 == 1]
    rank, room = [0] * n, [0] * n
    for r, q in enumerate(full + rest):
        rank[2 * q], rank[2 * q + 1] = r, n - 1 - r
        room[2 * q] = slots if q in full else -(-slots * 3 // 4)
        room[2 * q + 1] = -(-slots * 5 // 8)
    return rank, room


def level(device):
    chip = device // 2
    return jnp.where(device % 2 == 1, 2, (chip // 2 + chip) % 2)


def counts_kernel(n, mine_ref, all_ref, send_sem, recv_sem, own_sem):
    me = lax.axis_index("aux")
    greet([lax.rem(me + d, n) for d in range(1, n)])
    copies = [
        pltpu.make_async_remote_copy(
            src_ref=mine_ref,
            dst_ref=all_ref.at[me],
            send_sem=send_sem.at[d],
            recv_sem=recv_sem.at[d],
            device_id={"aux": lax.rem(me + d, n)},
            device_id_type=MESH,
        )
        for d in range(1, n)
    ]
    for one in copies:
        one.start()
    own = pltpu.make_async_copy(mine_ref, all_ref.at[me], own_sem)
    own.start()
    own.wait()
    for one in copies:
        one.wait()


def gather_counts(n, mine):
    return pl.pallas_call(
        functools.partial(counts_kernel, n),
        out_shape=jax.ShapeDtypeStruct((n,) + mine.shape, mine.dtype),
        in_specs=[VMEM],
        out_specs=VMEM,
        scratch_shapes=[
            pltpu.SemaphoreType.DMA((n,)),
            pltpu.SemaphoreType.DMA((n,)),
            pltpu.SemaphoreType.DMA,
        ],
        compiler_params=pltpu.CompilerParams(
            collective_id=3, has_side_effects=True, vmem_limit_bytes=4 * 2**20
        ),
    )(mine)


def exchange_kernel(
    n, slots, kinds, idx_ref, vals_ref, code_ref, out_ref, code_out,
    packed, send_sem, recv_sem, csend_sem, crecv_sem, own_sem,
):
    me = lax.axis_index("aux")
    greet([lax.rem(me + d, n) for d in range(1, n)])

    def values(d, count):
        peer = lax.rem(me + d, n)
        return pltpu.make_async_remote_copy(
            src_ref=packed.at[peer, pl.ds(0, count)],
            dst_ref=out_ref.at[me, pl.ds(0, count)],
            send_sem=send_sem.at[d],
            recv_sem=recv_sem.at[d],
            device_id={"aux": peer},
            device_id_type=MESH,
        )

    def codes(d):
        peer = lax.rem(me + d, n)
        return pltpu.make_async_remote_copy(
            src_ref=code_ref.at[peer],
            dst_ref=code_out.at[me],
            send_sem=csend_sem.at[d],
            recv_sem=crecv_sem.at[d],
            device_id={"aux": peer},
            device_id_type=MESH,
        )

    def by_kind(device, act):
        if len(kinds) == 1:
            act(kinds[0])
            return
        kind = level(device)
        for number, count in enumerate(kinds):
            pl.when(kind == number)(functools.partial(act, count))

    def pack(peer):
        for k in range(slots):
            packed[peer, k] = vals_ref[idx_ref[peer * slots + k]]

    def send(d, carry):
        peer = lax.rem(me + d, n)
        pack(peer)
        codes(d).start()
        by_kind(peer, lambda count: values(d, count).start())
        return carry

    lax.fori_loop(1, n, send, 0)
    pack(me)
    own_values = pltpu.make_async_copy(packed.at[me], out_ref.at[me], own_sem.at[0])
    own_codes = pltpu.make_async_copy(code_ref.at[me], code_out.at[me], own_sem.at[1])
    own_values.start()
    own_codes.start()
    own_values.wait()
    own_codes.wait()

    def finish(d, carry):
        codes(d).wait()
        by_kind(lax.rem(me + d, n), lambda count: values(d, count).wait_send())
        by_kind(me, lambda count: values(d, count).wait_recv())
        return carry

    lax.fori_loop(1, n, finish, 0)


def exchange(n, slots, kinds, number, idx, vals, codes):
    side = vals.shape[1]
    return pl.pallas_call(
        functools.partial(exchange_kernel, n, slots, kinds),
        out_shape=(
            jax.ShapeDtypeStruct((n, slots, side, side), vals.dtype),
            jax.ShapeDtypeStruct(codes.shape, codes.dtype),
        ),
        in_specs=[SMEM, VMEM, VMEM],
        out_specs=(ANY, ANY),
        scratch_shapes=[
            pltpu.VMEM((n, slots, side, side), vals.dtype),
            pltpu.SemaphoreType.DMA((n,)),
            pltpu.SemaphoreType.DMA((n,)),
            pltpu.SemaphoreType.DMA((n,)),
            pltpu.SemaphoreType.DMA((n,)),
            pltpu.SemaphoreType.DMA((2,)),
        ],
        compiler_params=pltpu.CompilerParams(
            collective_id=number, has_side_effects=True, vmem_limit_bytes=24 * 2**20
        ),
    )(idx, vals, codes)


def tile_kernel(n, slots, code_ref, vals_ref, coef_ref, out_ref, acc, seen):
    side = vals_ref.shape[1]
    mid = MU // 2

    def reset(key, carry):
        seen[key] = 0
        return carry

    lax.fori_loop(0, KEYS + 1, reset, 0)

    def add(step, carry):
        for k in range(slots):
            s = step * slots + k
            code = code_ref[s]
            key = jnp.where(code >= 0, code % KEYS, KEYS)
            col = jnp.where(code >= 0, code // KEYS, 0)
            part = jnp.dot(vals_ref[s], coef_ref[col], preferred_element_type=jnp.float32)
            rows = pl.ds(pl.multiple_of(key % ROW_BLKS * side, side), side)
            before = jnp.where(seen[key] == 1, acc[key // ROW_BLKS, rows, :], 0.0)
            acc[key // ROW_BLKS, rows, :] = before + part
            seen[key] = 1
        return carry

    lax.fori_loop(0, n, add, 0)
    out_ref[...] = jnp.zeros_like(out_ref)

    def against(left, right):
        return lax.dot_general(
            left, right, (((1,), (1,)), ((), ())), preferred_element_type=jnp.float32
        )

    def rounded(a):
        return jnp.concatenate(
            [
                jnp.where(
                    seen[a * ROW_BLKS + r] == 1, acc[a, r * side : (r + 1) * side, :], 0.0
                ).astype(jnp.bfloat16)
                for r in range(ROW_BLKS)
            ],
            axis=0,
        )

    def square(step, carry):
        h, g = rounded(2 * step), rounded(2 * step + 1)
        out_ref[:mid, :] += against(h[:mid], h) + against(g[:mid], g)
        out_ref[mid:, mid:] += against(h[mid:], h[mid:]) + against(g[mid:], g[mid:])
        return carry

    lax.fori_loop(0, AUX_DEV // 2, square, 0)
    out_ref[mid:, :mid] = out_ref[:mid, mid:].T


def tile(n, slots, codes, vals, coef):
    nocc = coef.shape[2]
    return pl.pallas_call(
        functools.partial(tile_kernel, n, slots),
        out_shape=jax.ShapeDtypeStruct((MU, MU), jnp.float32),
        in_specs=[SMEM, VMEM, VMEM],
        out_specs=VMEM,
        scratch_shapes=[
            pltpu.VMEM((AUX_DEV + 1, MU, nocc), jnp.float32),
            pltpu.SMEM((KEYS + 1,), jnp.int32),
        ],
        compiler_params=pltpu.CompilerParams(vmem_limit_bytes=56 * 2**20),
    )(codes, vals, coef)


def reduce_kernel(n, scale, k_ref, out_ref, got1, sum1, got2, sum2, got3, send_sem, recv_sem):
    me = lax.axis_index("aux")
    far = n // 4
    c, y, z = me % 2, me // 2 % 2, me // 4
    pair, side = me + 1 - 2 * c, me + 2 - 4 * y
    order = list(range(far - 1, -1, -1))
    chunk = [paired(z, t, far) for t in range(far)]
    greet([pair, side] + [me + 4 * (chunk[t] - z) for t in range(1, far)])

    def copy(src, dst, sem, other):
        return pltpu.make_async_remote_copy(
            src_ref=src,
            dst_ref=dst,
            send_sem=send_sem.at[sem],
            recv_sem=recv_sem.at[sem],
            device_id={"aux": other},
            device_id_type=MESH,
        )

    def across(t, half, sem):
        spot = chunk[t]
        return copy(k_ref.at[spot, half, 1 - c], got1.at[spot, half], sem, pair)

    give = [across(t, 1 - y, t) for t in range(far)]
    keep = [across(t, y, far + t) for t in range(far)]
    beside = [copy(sum1.at[t], got2.at[t], 2 * far + t, side) for t in range(far)]
    along = [
        copy(sum2.at[t], got3.at[t], 3 * far + t, me + 4 * (chunk[t] - z)) for t in range(far)
    ]
    for t in order:
        give[t].start()
    for t in order:
        keep[t].start()
    for t in order:
        give[t].wait()
        sum1[t] = k_ref[chunk[t], 1 - y, c] + got1[chunk[t], 1 - y]
        beside[t].start()
    for t in order:
        keep[t].wait()
        mine = k_ref[chunk[t], y, c] + got1[chunk[t], y]
        beside[t].wait()
        sum2[t] = mine + got2[t]
        if t:
            along[t].start()
    total = sum2[0]
    for t in order[:-1]:
        along[t].wait()
        total = total + got3[t]
    out_ref[...] = total * scale


def reduce_tile(n, scale, whole):
    far, rows = n // 4, MU // n
    f32 = jnp.float32
    return pl.pallas_call(
        functools.partial(reduce_kernel, n, scale),
        out_shape=jax.ShapeDtypeStruct((rows, MU), f32),
        in_specs=[VMEM],
        out_specs=VMEM,
        scratch_shapes=[
            pltpu.VMEM((far, 2, rows, MU), f32),
            pltpu.VMEM((far, rows, MU), f32),
            pltpu.VMEM((far, rows, MU), f32),
            pltpu.VMEM((far, rows, MU), f32),
            pltpu.VMEM((far, rows, MU), f32),
            pltpu.SemaphoreType.DMA((4 * far,)),
            pltpu.SemaphoreType.DMA((4 * far,)),
        ],
        compiler_params=pltpu.CompilerParams(
            collective_id=1, has_side_effects=True, vmem_limit_bytes=6 * 2**20
        ),
    )(whole.reshape(far, 2, 2, rows, MU))


def body(block_values, block_dest, block_aux, block_row, block_col, coefficients):
    n = lax.axis_size("aux")
    count, side = block_values.shape[:2]
    nocc = coefficients.shape[1]
    slots = 2 * count // n
    dest = block_dest[:, 0]
    rank_of, room = spread(n, slots)
    tiered = min(room) < slots
    if tiered:
        named = dest[:, None] == jnp.arange(128, dtype=jnp.int32)[None, :]
        mine = jnp.sum(named.astype(jnp.int32), axis=0)
        counts = gather_counts(n, jnp.broadcast_to(mine[None, :], (8, 128)))[:, 0, :n]
        most = jnp.max(counts, axis=0)
        score = (most * 4096 + jnp.sum(counts, axis=0)) * n - jnp.arange(n, dtype=jnp.int32)
        rank = jnp.sum((score[None, :] > score[:, None]).astype(jnp.int32), axis=1)
        lies = rank[:, None] == jnp.asarray(rank_of, jnp.int32)[None, :]
        device = jnp.sum(jnp.where(lies, jnp.arange(n, dtype=jnp.int32)[None, :], 0), axis=1)
        fits = jnp.all(jnp.where(lies, jnp.asarray(room, jnp.int32)[None, :] >= most[:, None], True))
        dest = jnp.sum(jnp.where(named[:, :n], device[None, :], 0), axis=1)
    place = jnp.arange(count, dtype=jnp.int32)
    earlier = (dest[:, None] == dest[None, :]) & (place[:, None] > place[None, :])
    target = dest * slots + jnp.sum(earlier.astype(jnp.int32), axis=1)
    hit = target[None, :] == jnp.arange(n * slots, dtype=jnp.int32)[:, None]
    idx = jnp.sum(jnp.where(hit, place[None, :], 0), axis=1)
    code = block_col * KEYS + block_aux * ROW_BLKS + block_row
    sent = jnp.sum(jnp.where(hit, code[None, :] + 1, 0), axis=1) - 1
    sent = jnp.pad(sent.reshape(n, 1, slots), ((0, 0), (0, 7), (0, 128 - slots)))
    if tiered:
        kinds = (room[0], room[2], room[1])
        values, codes = lax.cond(
            fits,
            functools.partial(exchange, n, slots, kinds, 0),
            functools.partial(exchange, n, slots, (slots,), 2),
            idx,
            block_values,
            sent,
        )
    else:
        values, codes = exchange(n, slots, (slots,), 2, idx, block_values, sent)
    whole = tile(
        n,
        slots,
        codes[:, 0, :slots].reshape(n * slots),
        values.reshape(n * slots, side, side),
        coefficients.reshape(-1, side, nocc),
    )
    return reduce_tile(n, 1.0 / nocc, whole)


def solution(mesh):
    placed = (
        P(("grp", "aux"), None, None),
        P(("grp", "aux"), None),
        P(("grp", "aux")),
        P(("grp", "aux")),
        P(("grp", "aux")),
        P("grp", None),
    )
    return jax.shard_map(
        body, mesh=mesh, in_specs=placed, out_specs=P(("grp", "aux"), None), check_vma=False
    )
```

```python
import functools

import jax
import jax.numpy as jnp
from jax import lax
from jax.experimental import pallas as pl
from jax.experimental.pallas import tpu as pltpu
from jax.sharding import PartitionSpec as P

ROW_BLKS = 4
AUX_DEV = 16
KEYS = ROW_BLKS * AUX_DEV
MU = 512
MESH = pl.DeviceIdType.MESH
VMEM = pl.BlockSpec(memory_space=pltpu.VMEM)
SMEM = pl.BlockSpec(memory_space=pltpu.SMEM)
ANY = pl.BlockSpec(memory_space=pl.ANY)


def paired(me, d, n):
    peer, bit = 0, 1
    while bit < n:
        mine, other = me // bit % 2, d // bit % 2
        peer = peer + bit * (mine + other - 2 * mine * other)
        bit *= 2
    return peer


def greet(others):
    barrier = pltpu.get_barrier_semaphore()
    for other in others:
        pl.semaphore_signal(barrier, inc=1, device_id={"aux": other}, device_id_type=MESH)
    pl.semaphore_wait(barrier, len(others))


def spread(n, slots):
    chips = n // 2
    full = [q for q in range(chips) if (q // 2 + q) % 2 == 0]
    rest = [q for q in range(chips) if (q // 2 + q) % 2 == 1]
    rank, room = [0] * n, [0] * n
    for r, q in enumerate(full + rest):
        rank[2 * q], rank[2 * q + 1] = r, n - 1 - r
        room[2 * q] = slots if q in full else -(-slots * 3 // 4)
        room[2 * q + 1] = -(-slots * 5 // 8)
    return rank, room


def level(device):
    chip = device // 2
    return jnp.where(device % 2 == 1, 2, (chip // 2 + chip) % 2)


def counts_kernel(n, mine_ref, all_ref, send_sem, recv_sem, own_sem):
    me = lax.axis_index("aux")
    greet([lax.rem(me + d, n) for d in range(1, n)])
    copies = [
        pltpu.make_async_remote_copy(
            src_ref=mine_ref,
            dst_ref=all_ref.at[me],
            send_sem=send_sem.at[d],
            recv_sem=recv_sem.at[d],
            device_id={"aux": lax.rem(me + d, n)},
            device_id_type=MESH,
        )
        for d in range(1, n)
    ]
    for one in copies:
        one.start()
    own = pltpu.make_async_copy(mine_ref, all_ref.at[me], own_sem)
    own.start()
    own.wait()
    for one in copies:
        one.wait()


def gather_counts(n, mine):
    return pl.pallas_call(
        functools.partial(counts_kernel, n),
        out_shape=jax.ShapeDtypeStruct((n,) + mine.shape, mine.dtype),
        in_specs=[VMEM],
        out_specs=VMEM,
        scratch_shapes=[
            pltpu.SemaphoreType.DMA((n,)),
            pltpu.SemaphoreType.DMA((n,)),
            pltpu.SemaphoreType.DMA,
        ],
        compiler_params=pltpu.CompilerParams(
            collective_id=3, has_side_effects=True, vmem_limit_bytes=4 * 2**20
        ),
    )(mine)


def exchange_kernel(
    n, slots, kinds, idx_ref, vals_ref, code_ref, out_ref, code_out,
    packed, send_sem, recv_sem, csend_sem, crecv_sem, own_sem,
):
    me = lax.axis_index("aux")
    greet([lax.rem(me + d, n) for d in range(1, n)])

    turn = jnp.where(me < n // 2, n - 1, 1)

    def values(peer, count, sem):
        return pltpu.make_async_remote_copy(
            src_ref=packed.at[peer, pl.ds(0, count)],
            dst_ref=out_ref.at[me, pl.ds(0, count)],
            send_sem=send_sem.at[peer],
            recv_sem=recv_sem.at[sem],
            device_id={"aux": peer},
            device_id_type=MESH,
        )

    def codes(peer, sem):
        return pltpu.make_async_remote_copy(
            src_ref=code_ref.at[peer],
            dst_ref=code_out.at[me],
            send_sem=csend_sem.at[peer],
            recv_sem=crecv_sem.at[sem],
            device_id={"aux": peer},
            device_id_type=MESH,
        )

    def by_kind(device, act):
        if len(kinds) == 1:
            act(kinds[0])
            return
        kind = level(device)
        for number, count in enumerate(kinds):
            pl.when(kind == number)(functools.partial(act, count))

    def pack(peer):
        for k in range(slots):
            packed[peer, k] = vals_ref[idx_ref[peer * slots + k]]

    def send(d, carry):
        peer = lax.rem(me + d * turn, n)
        pack(peer)
        codes(peer, me).start()
        by_kind(peer, lambda count: values(peer, count, me).start())
        return carry

    lax.fori_loop(1, n, send, 0)
    pack(me)
    own_values = pltpu.make_async_copy(packed.at[me], out_ref.at[me], own_sem.at[0])
    own_codes = pltpu.make_async_copy(code_ref.at[me], code_out.at[me], own_sem.at[1])
    own_values.start()
    own_codes.start()
    own_values.wait()
    own_codes.wait()

    def finish(d, carry):
        peer = lax.rem(me + d * turn, n)
        codes(peer, peer).wait()
        by_kind(peer, lambda count: values(peer, count, me).wait_send())
        by_kind(me, lambda count: values(peer, count, peer).wait_recv())
        return carry

    lax.fori_loop(1, n, finish, 0)


def exchange(n, slots, kinds, number, idx, vals, codes):
    side = vals.shape[1]
    return pl.pallas_call(
        functools.partial(exchange_kernel, n, slots, kinds),
        out_shape=(
            jax.ShapeDtypeStruct((n, slots, side, side), vals.dtype),
            jax.ShapeDtypeStruct(codes.shape, codes.dtype),
        ),
        in_specs=[SMEM, VMEM, VMEM],
        out_specs=(ANY, ANY),
        scratch_shapes=[
            pltpu.VMEM((n, slots, side, side), vals.dtype),
            pltpu.SemaphoreType.DMA((n,)),
            pltpu.SemaphoreType.DMA((n,)),
            pltpu.SemaphoreType.DMA((n,)),
            pltpu.SemaphoreType.DMA((n,)),
            pltpu.SemaphoreType.DMA((2,)),
        ],
        compiler_params=pltpu.CompilerParams(
            collective_id=number, has_side_effects=True, vmem_limit_bytes=24 * 2**20
        ),
    )(idx, vals, codes)


def tile_kernel(n, slots, code_ref, vals_ref, coef_ref, out_ref, acc, seen):
    side = vals_ref.shape[1]
    mid = MU // 2

    def reset(key, carry):
        seen[key] = 0
        return carry

    lax.fori_loop(0, KEYS + 1, reset, 0)

    def add(step, carry):
        for k in range(slots):
            s = step * slots + k
            code = code_ref[s]
            key = jnp.where(code >= 0, code % KEYS, KEYS)
            col = jnp.where(code >= 0, code // KEYS, 0)
            part = jnp.dot(vals_ref[s], coef_ref[col], preferred_element_type=jnp.float32)
            rows = pl.ds(pl.multiple_of(key % ROW_BLKS * side, side), side)
            before = jnp.where(seen[key] == 1, acc[key // ROW_BLKS, rows, :], 0.0)
            acc[key // ROW_BLKS, rows, :] = before + part
            seen[key] = 1
        return carry

    lax.fori_loop(0, n, add, 0)
    out_ref[...] = jnp.zeros_like(out_ref)

    def against(left, right):
        return lax.dot_general(
            left, right, (((1,), (1,)), ((), ())), preferred_element_type=jnp.float32
        )

    def rounded(a):
        return jnp.concatenate(
            [
                jnp.where(
                    seen[a * ROW_BLKS + r] == 1, acc[a, r * side : (r + 1) * side, :], 0.0
                ).astype(jnp.bfloat16)
                for r in range(ROW_BLKS)
            ],
            axis=0,
        )

    def square(step, carry):
        h, g = rounded(2 * step), rounded(2 * step + 1)
        out_ref[:mid, :] += against(h[:mid], h) + against(g[:mid], g)
        out_ref[mid:, mid:] += against(h[mid:], h[mid:]) + against(g[mid:], g[mid:])
        return carry

    lax.fori_loop(0, AUX_DEV // 2, square, 0)
    out_ref[mid:, :mid] = out_ref[:mid, mid:].T


def tile(n, slots, codes, vals, coef):
    nocc = coef.shape[2]
    return pl.pallas_call(
        functools.partial(tile_kernel, n, slots),
        out_shape=jax.ShapeDtypeStruct((MU, MU), jnp.float32),
        in_specs=[SMEM, VMEM, VMEM],
        out_specs=VMEM,
        scratch_shapes=[
            pltpu.VMEM((AUX_DEV + 1, MU, nocc), jnp.float32),
            pltpu.SMEM((KEYS + 1,), jnp.int32),
        ],
        compiler_params=pltpu.CompilerParams(vmem_limit_bytes=56 * 2**20),
    )(codes, vals, coef)


def reduce_kernel(n, scale, k_ref, out_ref, got1, sum1, got2, sum2, got3, send_sem, recv_sem):
    me = lax.axis_index("aux")
    far = n // 4
    c, y, z = me % 2, me // 2 % 2, me // 4
    pair, side = me + 1 - 2 * c, me + 2 - 4 * y
    order = list(range(far - 1, -1, -1))
    chunk = [paired(z, t, far) for t in range(far)]
    greet([pair, side] + [me + 4 * (chunk[t] - z) for t in range(1, far)])

    def copy(src, dst, sem, other):
        return pltpu.make_async_remote_copy(
            src_ref=src,
            dst_ref=dst,
            send_sem=send_sem.at[sem],
            recv_sem=recv_sem.at[sem],
            device_id={"aux": other},
            device_id_type=MESH,
        )

    def across(t, half, sem):
        spot = chunk[t]
        return copy(k_ref.at[spot, half, 1 - c], got1.at[spot, half], sem, pair)

    give = [across(t, 1 - y, t) for t in range(far)]
    keep = [across(t, y, far + t) for t in range(far)]
    beside = [copy(sum1.at[t], got2.at[t], 2 * far + t, side) for t in range(far)]
    along = [
        copy(sum2.at[t], got3.at[t], 3 * far + t, me + 4 * (chunk[t] - z)) for t in range(far)
    ]
    for t in order:
        give[t].start()
    for t in order:
        keep[t].start()
    for t in order:
        give[t].wait()
        sum1[t] = k_ref[chunk[t], 1 - y, c] + got1[chunk[t], 1 - y]
        beside[t].start()
    for t in order:
        keep[t].wait()
        mine = k_ref[chunk[t], y, c] + got1[chunk[t], y]
        beside[t].wait()
        sum2[t] = mine + got2[t]
        if t:
            along[t].start()
    total = sum2[0]
    for t in order[:-1]:
        along[t].wait()
        total = total + got3[t]
    out_ref[...] = total * scale


def reduce_tile(n, scale, whole):
    far, rows = n // 4, MU // n
    f32 = jnp.float32
    return pl.pallas_call(
        functools.partial(reduce_kernel, n, scale),
        out_shape=jax.ShapeDtypeStruct((rows, MU), f32),
        in_specs=[VMEM],
        out_specs=VMEM,
        scratch_shapes=[
            pltpu.VMEM((far, 2, rows, MU), f32),
            pltpu.VMEM((far, rows, MU), f32),
            pltpu.VMEM((far, rows, MU), f32),
            pltpu.VMEM((far, rows, MU), f32),
            pltpu.VMEM((far, rows, MU), f32),
            pltpu.SemaphoreType.DMA((4 * far,)),
            pltpu.SemaphoreType.DMA((4 * far,)),
        ],
        compiler_params=pltpu.CompilerParams(
            collective_id=1, has_side_effects=True, vmem_limit_bytes=6 * 2**20
        ),
    )(whole.reshape(far, 2, 2, rows, MU))


def body(block_values, block_dest, block_aux, block_row, block_col, coefficients):
    n = lax.axis_size("aux")
    count, side = block_values.shape[:2]
    nocc = coefficients.shape[1]
    slots = 2 * count // n
    dest = block_dest[:, 0]
    rank_of, room = spread(n, slots)
    tiered = min(room) < slots
    if tiered:
        named = dest[:, None] == jnp.arange(128, dtype=jnp.int32)[None, :]
        mine = jnp.sum(named.astype(jnp.int32), axis=0)
        counts = gather_counts(n, jnp.broadcast_to(mine[None, :], (8, 128)))[:, 0, :n]
        most = jnp.max(counts, axis=0)
        score = (most * 4096 + jnp.sum(counts, axis=0)) * n - jnp.arange(n, dtype=jnp.int32)
        rank = jnp.sum((score[None, :] > score[:, None]).astype(jnp.int32), axis=1)
        lies = rank[:, None] == jnp.asarray(rank_of, jnp.int32)[None, :]
        device = jnp.sum(jnp.where(lies, jnp.arange(n, dtype=jnp.int32)[None, :], 0), axis=1)
        fits = jnp.all(jnp.where(lies, jnp.asarray(room, jnp.int32)[None, :] >= most[:, None], True))
        dest = jnp.sum(jnp.where(named[:, :n], device[None, :], 0), axis=1)
    place = jnp.arange(count, dtype=jnp.int32)
    earlier = (dest[:, None] == dest[None, :]) & (place[:, None] > place[None, :])
    target = dest * slots + jnp.sum(earlier.astype(jnp.int32), axis=1)
    hit = target[None, :] == jnp.arange(n * slots, dtype=jnp.int32)[:, None]
    idx = jnp.sum(jnp.where(hit, place[None, :], 0), axis=1)
    code = block_col * KEYS + block_aux * ROW_BLKS + block_row
    sent = jnp.sum(jnp.where(hit, code[None, :] + 1, 0), axis=1) - 1
    sent = jnp.pad(sent.reshape(n, 1, slots), ((0, 0), (0, 7), (0, 128 - slots)))
    if tiered:
        kinds = (room[0], room[2], room[1])
        values, codes = lax.cond(
            fits,
            functools.partial(exchange, n, slots, kinds, 0),
            functools.partial(exchange, n, slots, (slots,), 2),
            idx,
            block_values,
            sent,
        )
    else:
        values, codes = exchange(n, slots, (slots,), 2, idx, block_values, sent)
    whole = tile(
        n,
        slots,
        codes[:, 0, :slots].reshape(n * slots),
        values.reshape(n * slots, side, side),
        coefficients.reshape(-1, side, nocc),
    )
    return reduce_tile(n, 1.0 / nocc, whole)


def solution(mesh):
    placed = (
        P(("grp", "aux"), None, None),
        P(("grp", "aux"), None),
        P(("grp", "aux")),
        P(("grp", "aux")),
        P(("grp", "aux")),
        P("grp", None),
    )
    return jax.shard_map(
        body, mesh=mesh, in_specs=placed, out_specs=P(("grp", "aux"), None), check_vma=False
    )
```

```python
import functools

import jax
import jax.numpy as jnp
from jax import lax
from jax.experimental import pallas as pl
from jax.experimental.pallas import tpu as pltpu
from jax.sharding import PartitionSpec as P

ROW_BLKS = 4
AUX_DEV = 16
KEYS = ROW_BLKS * AUX_DEV
MU = 512
MESH = pl.DeviceIdType.MESH
VMEM = pl.BlockSpec(memory_space=pltpu.VMEM)
SMEM = pl.BlockSpec(memory_space=pltpu.SMEM)
ANY = pl.BlockSpec(memory_space=pl.ANY)


def paired(me, d, n):
    peer, bit = 0, 1
    while bit < n:
        mine, other = me // bit % 2, d // bit % 2
        peer = peer + bit * (mine + other - 2 * mine * other)
        bit *= 2
    return peer


def greet(others):
    barrier = pltpu.get_barrier_semaphore()
    for other in others:
        pl.semaphore_signal(barrier, inc=1, device_id={"aux": other}, device_id_type=MESH)
    pl.semaphore_wait(barrier, len(others))


def spread(n, slots):
    chips = n // 2
    full = [q for q in range(chips) if (q // 2 + q) % 2 == 0]
    rest = [q for q in range(chips) if (q // 2 + q) % 2 == 1]
    rank, room = [0] * n, [0] * n
    for r, q in enumerate(full + rest):
        rank[2 * q], rank[2 * q + 1] = r, n - 1 - r
        room[2 * q] = slots if q in full else -(-slots * 3 // 4)
        room[2 * q + 1] = -(-slots * 5 // 8)
    return rank, room


def level(device):
    chip = device // 2
    return jnp.where(device % 2 == 1, 2, (chip // 2 + chip) % 2)


def counts_kernel(n, mine_ref, all_ref, send_sem, recv_sem, own_sem):
    me = lax.axis_index("aux")
    greet([lax.rem(me + d, n) for d in range(1, n)])
    copies = [
        pltpu.make_async_remote_copy(
            src_ref=mine_ref,
            dst_ref=all_ref.at[me],
            send_sem=send_sem.at[d],
            recv_sem=recv_sem.at[d],
            device_id={"aux": lax.rem(me + d, n)},
            device_id_type=MESH,
        )
        for d in range(1, n)
    ]
    for one in copies:
        one.start()
    own = pltpu.make_async_copy(mine_ref, all_ref.at[me], own_sem)
    own.start()
    own.wait()
    for one in copies:
        one.wait()


def gather_counts(n, mine):
    return pl.pallas_call(
        functools.partial(counts_kernel, n),
        out_shape=jax.ShapeDtypeStruct((n,) + mine.shape, mine.dtype),
        in_specs=[VMEM],
        out_specs=VMEM,
        scratch_shapes=[
            pltpu.SemaphoreType.DMA((n,)),
            pltpu.SemaphoreType.DMA((n,)),
            pltpu.SemaphoreType.DMA,
        ],
        compiler_params=pltpu.CompilerParams(
            collective_id=3, has_side_effects=True, vmem_limit_bytes=4 * 2**20
        ),
    )(mine)


def exchange_kernel(
    n, slots, kinds, idx_ref, vals_ref, code_ref, out_ref, code_out,
    packed, send_sem, recv_sem, csend_sem, crecv_sem, own_sem,
):
    me = lax.axis_index("aux")
    greet([lax.rem(me + d, n) for d in range(1, n)])

    def partner(step):
        at = step - 1
        crossing = ((at + me) % 2 == 0) | (at == n - 2)
        return paired(me, jnp.where(crossing, n - 1, n // 2 - 1) - at // 2, n)

    def values(peer, count, sem):
        return pltpu.make_async_remote_copy(
            src_ref=packed.at[peer, pl.ds(0, count)],
            dst_ref=out_ref.at[me, pl.ds(0, count)],
            send_sem=send_sem.at[peer],
            recv_sem=recv_sem.at[sem],
            device_id={"aux": peer},
            device_id_type=MESH,
        )

    def codes(peer, sem):
        return pltpu.make_async_remote_copy(
            src_ref=code_ref.at[peer],
            dst_ref=code_out.at[me],
            send_sem=csend_sem.at[peer],
            recv_sem=crecv_sem.at[sem],
            device_id={"aux": peer},
            device_id_type=MESH,
        )

    def by_kind(device, act):
        if len(kinds) == 1:
            act(kinds[0])
            return
        kind = level(device)
        for number, count in enumerate(kinds):
            pl.when(kind == number)(functools.partial(act, count))

    def pack(peer):
        for k in range(slots):
            packed[peer, k] = vals_ref[idx_ref[peer * slots + k]]

    def send(d, carry):
        peer = partner(d)
        pack(peer)
        codes(peer, me).start()
        by_kind(peer, lambda count: values(peer, count, me).start())
        return carry

    lax.fori_loop(1, n, send, 0)
    pack(me)
    own_values = pltpu.make_async_copy(packed.at[me], out_ref.at[me], own_sem.at[0])
    own_codes = pltpu.make_async_copy(code_ref.at[me], code_out.at[me], own_sem.at[1])
    own_values.start()
    own_codes.start()
    own_values.wait()
    own_codes.wait()

    def finish(d, carry):
        peer = partner(d)
        codes(peer, peer).wait()
        by_kind(peer, lambda count: values(peer, count, me).wait_send())
        by_kind(me, lambda count: values(peer, count, peer).wait_recv())
        return carry

    lax.fori_loop(1, n, finish, 0)


def exchange(n, slots, kinds, number, idx, vals, codes):
    side = vals.shape[1]
    return pl.pallas_call(
        functools.partial(exchange_kernel, n, slots, kinds),
        out_shape=(
            jax.ShapeDtypeStruct((n, slots, side, side), vals.dtype),
            jax.ShapeDtypeStruct(codes.shape, codes.dtype),
        ),
        in_specs=[SMEM, VMEM, VMEM],
        out_specs=(ANY, ANY),
        scratch_shapes=[
            pltpu.VMEM((n, slots, side, side), vals.dtype),
            pltpu.SemaphoreType.DMA((n,)),
            pltpu.SemaphoreType.DMA((n,)),
            pltpu.SemaphoreType.DMA((n,)),
            pltpu.SemaphoreType.DMA((n,)),
            pltpu.SemaphoreType.DMA((2,)),
        ],
        compiler_params=pltpu.CompilerParams(
            collective_id=number, has_side_effects=True, vmem_limit_bytes=24 * 2**20
        ),
    )(idx, vals, codes)


def tile_kernel(
    n, slots, wide, code_ref, vals_hbm, coef_hbm, out_ref, vals_ref, coef_ref, acc, seen, sem
):
    side = vals_ref.shape[1]
    mid = MU // 2
    parts = coef_ref.shape[2] // wide

    def coef_copy(j):
        columns = pl.ds(j * wide, wide)
        return pltpu.make_async_copy(
            coef_hbm.at[:, :, columns], coef_ref.at[:, :, columns], sem.at[n + j]
        )

    def vals_copy(p):
        rows = pl.ds(p * slots, slots)
        return pltpu.make_async_copy(vals_hbm.at[rows], vals_ref.at[rows], sem.at[p])

    coef_copy(0).start()
    for p in range(n):
        vals_copy(p).start()
    for j in range(1, parts):
        coef_copy(j).start()

    def reset(key, carry):
        seen[key] = 0
        return carry

    lax.fori_loop(0, KEYS + 1, reset, 0)

    for j in range(parts):
        coef_copy(j).wait()
        columns = pl.ds(j * wide, wide)

        def add(step, carry):
            if j == 0:
                vals_copy(step).wait()
            for k in range(slots):
                s = step * slots + k
                code = code_ref[s]
                key = jnp.where(code >= 0, code % KEYS, KEYS)
                col = jnp.where(code >= 0, code // KEYS, 0)
                part = jnp.dot(
                    vals_ref[s], coef_ref[col, :, columns], preferred_element_type=jnp.float32
                )
                rows = pl.ds(pl.multiple_of(key % ROW_BLKS * side, side), side)
                begun = seen[key] == j + 1
                before = jnp.where(begun, acc[key // ROW_BLKS, rows, columns], 0.0)
                acc[key // ROW_BLKS, rows, columns] = before + part
                seen[key] = j + 1
            return carry

        lax.fori_loop(0, n, add, 0)

    out_ref[...] = jnp.zeros_like(out_ref)

    def against(left, right):
        return lax.dot_general(
            left, right, (((1,), (1,)), ((), ())), preferred_element_type=jnp.float32
        )

    def rounded(a):
        return jnp.concatenate(
            [
                jnp.where(
                    seen[a * ROW_BLKS + r] > 0, acc[a, r * side : (r + 1) * side, :], 0.0
                ).astype(jnp.bfloat16)
                for r in range(ROW_BLKS)
            ],
            axis=0,
        )

    def square(step, carry):
        h, g = rounded(2 * step), rounded(2 * step + 1)
        out_ref[:mid, :] += against(h[:mid], h) + against(g[:mid], g)
        out_ref[mid:, mid:] += against(h[mid:], h[mid:]) + against(g[mid:], g[mid:])
        return carry

    lax.fori_loop(0, AUX_DEV // 2, square, 0)
    out_ref[mid:, :mid] = out_ref[:mid, mid:].T


def tile(n, slots, codes, vals, coef):
    nocc = coef.shape[2]
    wide = 256 if nocc % 256 == 0 else nocc
    return pl.pallas_call(
        functools.partial(tile_kernel, n, slots, wide),
        out_shape=jax.ShapeDtypeStruct((MU, MU), jnp.float32),
        in_specs=[SMEM, ANY, ANY],
        out_specs=VMEM,
        scratch_shapes=[
            pltpu.VMEM(vals.shape, vals.dtype),
            pltpu.VMEM(coef.shape, coef.dtype),
            pltpu.VMEM((AUX_DEV + 1, MU, nocc), jnp.float32),
            pltpu.SMEM((KEYS + 1,), jnp.int32),
            pltpu.SemaphoreType.DMA((n + nocc // wide,)),
        ],
        compiler_params=pltpu.CompilerParams(vmem_limit_bytes=56 * 2**20),
    )(codes, vals, coef)


def reduce_kernel(n, scale, k_ref, out_ref, got1, sum1, got2, sum2, got3, send_sem, recv_sem):
    me = lax.axis_index("aux")
    far = n // 4
    c, y, z = me % 2, me // 2 % 2, me // 4
    pair, side = me + 1 - 2 * c, me + 2 - 4 * y
    order = list(range(far - 1, -1, -1))
    chunk = [paired(z, t, far) for t in range(far)]
    greet([pair, side] + [me + 4 * (chunk[t] - z) for t in range(1, far)])

    def copy(src, dst, sem, other):
        return pltpu.make_async_remote_copy(
            src_ref=src,
            dst_ref=dst,
            send_sem=send_sem.at[sem],
            recv_sem=recv_sem.at[sem],
            device_id={"aux": other},
            device_id_type=MESH,
        )

    def across(t, half, sem):
        spot = chunk[t]
        return copy(k_ref.at[spot, half, 1 - c], got1.at[spot, half], sem, pair)

    give = [across(t, 1 - y, t) for t in range(far)]
    keep = [across(t, y, far + t) for t in range(far)]
    beside = [copy(sum1.at[t], got2.at[t], 2 * far + t, side) for t in range(far)]
    along = [
        copy(sum2.at[t], got3.at[t], 3 * far + t, me + 4 * (chunk[t] - z)) for t in range(far)
    ]
    for t in order:
        give[t].start()
    for t in order:
        keep[t].start()
    for t in order:
        give[t].wait()
        sum1[t] = k_ref[chunk[t], 1 - y, c] + got1[chunk[t], 1 - y]
        beside[t].start()
    for t in order:
        keep[t].wait()
        mine = k_ref[chunk[t], y, c] + got1[chunk[t], y]
        beside[t].wait()
        sum2[t] = mine + got2[t]
        if t:
            along[t].start()
    total = sum2[0]
    for t in order[:-1]:
        along[t].wait()
        total = total + got3[t]
    out_ref[...] = total * scale


def reduce_tile(n, scale, whole):
    far, rows = n // 4, MU // n
    f32 = jnp.float32
    return pl.pallas_call(
        functools.partial(reduce_kernel, n, scale),
        out_shape=jax.ShapeDtypeStruct((rows, MU), f32),
        in_specs=[VMEM],
        out_specs=VMEM,
        scratch_shapes=[
            pltpu.VMEM((far, 2, rows, MU), f32),
            pltpu.VMEM((far, rows, MU), f32),
            pltpu.VMEM((far, rows, MU), f32),
            pltpu.VMEM((far, rows, MU), f32),
            pltpu.VMEM((far, rows, MU), f32),
            pltpu.SemaphoreType.DMA((4 * far,)),
            pltpu.SemaphoreType.DMA((4 * far,)),
        ],
        compiler_params=pltpu.CompilerParams(
            collective_id=1, has_side_effects=True, vmem_limit_bytes=6 * 2**20
        ),
    )(whole.reshape(far, 2, 2, rows, MU))


def body(block_values, block_dest, block_aux, block_row, block_col, coefficients):
    n = lax.axis_size("aux")
    count, side = block_values.shape[:2]
    nocc = coefficients.shape[1]
    slots = 2 * count // n
    dest = block_dest[:, 0]
    rank_of, room = spread(n, slots)
    tiered = min(room) < slots
    if tiered:
        named = dest[:, None] == jnp.arange(128, dtype=jnp.int32)[None, :]
        mine = jnp.sum(named.astype(jnp.int32), axis=0)
        counts = gather_counts(n, jnp.broadcast_to(mine[None, :], (8, 128)))[:, 0, :n]
        most = jnp.max(counts, axis=0)
        score = (most * 4096 + jnp.sum(counts, axis=0)) * n - jnp.arange(n, dtype=jnp.int32)
        rank = jnp.sum((score[None, :] > score[:, None]).astype(jnp.int32), axis=1)
        lies = rank[:, None] == jnp.asarray(rank_of, jnp.int32)[None, :]
        device = jnp.sum(jnp.where(lies, jnp.arange(n, dtype=jnp.int32)[None, :], 0), axis=1)
        fits = jnp.all(jnp.where(lies, jnp.asarray(room, jnp.int32)[None, :] >= most[:, None], True))
        dest = jnp.sum(jnp.where(named[:, :n], device[None, :], 0), axis=1)
    place = jnp.arange(count, dtype=jnp.int32)
    earlier = (dest[:, None] == dest[None, :]) & (place[:, None] > place[None, :])
    target = dest * slots + jnp.sum(earlier.astype(jnp.int32), axis=1)
    hit = target[None, :] == jnp.arange(n * slots, dtype=jnp.int32)[:, None]
    idx = jnp.sum(jnp.where(hit, place[None, :], 0), axis=1)
    code = block_col * KEYS + block_aux * ROW_BLKS + block_row
    sent = jnp.sum(jnp.where(hit, code[None, :] + 1, 0), axis=1) - 1
    sent = jnp.pad(sent.reshape(n, 1, slots), ((0, 0), (0, 7), (0, 128 - slots)))
    if tiered:
        kinds = (room[0], room[2], room[1])
        values, codes = lax.cond(
            fits,
            functools.partial(exchange, n, slots, kinds, 0),
            functools.partial(exchange, n, slots, (slots,), 2),
            idx,
            block_values,
            sent,
        )
    else:
        values, codes = exchange(n, slots, (slots,), 2, idx, block_values, sent)
    whole = tile(
        n,
        slots,
        codes[:, 0, :slots].reshape(n * slots),
        values.reshape(n * slots, side, side),
        coefficients.reshape(-1, side, nocc),
    )
    return reduce_tile(n, 1.0 / nocc, whole)


def solution(mesh):
    placed = (
        P(("grp", "aux"), None, None),
        P(("grp", "aux"), None),
        P(("grp", "aux")),
        P(("grp", "aux")),
        P(("grp", "aux")),
        P("grp", None),
    )
    return jax.shard_map(
        body, mesh=mesh, in_specs=placed, out_specs=P(("grp", "aux"), None), check_vma=False
    )
```

```python
import functools

import jax
import jax.numpy as jnp
from jax import lax
from jax.experimental import pallas as pl
from jax.experimental.pallas import tpu as pltpu
from jax.sharding import PartitionSpec as P

ROW_BLKS = 4
AUX_DEV = 16
KEYS = ROW_BLKS * AUX_DEV
MU = 512
MESH = pl.DeviceIdType.MESH
VMEM = pl.BlockSpec(memory_space=pltpu.VMEM)
SMEM = pl.BlockSpec(memory_space=pltpu.SMEM)
ANY = pl.BlockSpec(memory_space=pl.ANY)


def paired(me, d, n):
    peer, bit = 0, 1
    while bit < n:
        mine, other = me // bit % 2, d // bit % 2
        peer = peer + bit * (mine + other - 2 * mine * other)
        bit *= 2
    return peer


def greet(others):
    barrier = pltpu.get_barrier_semaphore()
    for other in others:
        pl.semaphore_signal(barrier, inc=1, device_id={"aux": other}, device_id_type=MESH)
    pl.semaphore_wait(barrier, len(others))


def level(device, n):
    chip = device // 2
    first, low = (chip // 2 + chip) % 2 == 0, chip < n // 4
    upper = jnp.where(first, jnp.where(low, 0, 1), 2)
    return jnp.where(device % 2 == 0, upper, jnp.where(first & low, 4, 3))


def spread(n, slots):
    chips = range(n // 2)
    order = [q for q in chips if (q // 2 + q) % 2 == 0] + [q for q in chips if (q // 2 + q) % 2]
    lies = [2 * q for q in order] + [2 * q + 1 for q in reversed(order)]
    return lies, tuple(-(-slots * eighths // 8) for eighths in (8, 7, 6, 5, 4))


def counts_kernel(n, mine_ref, all_ref, send_sem, recv_sem, own_sem):
    me = lax.axis_index("aux")
    greet([lax.rem(me + d, n) for d in range(1, n)])
    copies = [
        pltpu.make_async_remote_copy(
            src_ref=mine_ref,
            dst_ref=all_ref.at[me],
            send_sem=send_sem.at[d],
            recv_sem=recv_sem.at[d],
            device_id={"aux": lax.rem(me + d, n)},
            device_id_type=MESH,
        )
        for d in range(1, n)
    ]
    for one in copies:
        one.start()
    own = pltpu.make_async_copy(mine_ref, all_ref.at[me], own_sem)
    own.start()
    own.wait()
    for one in copies:
        one.wait()


def gather_counts(n, mine):
    return pl.pallas_call(
        functools.partial(counts_kernel, n),
        out_shape=jax.ShapeDtypeStruct((n,) + mine.shape, mine.dtype),
        in_specs=[VMEM],
        out_specs=VMEM,
        scratch_shapes=[
            pltpu.SemaphoreType.DMA((n,)),
            pltpu.SemaphoreType.DMA((n,)),
            pltpu.SemaphoreType.DMA,
        ],
        compiler_params=pltpu.CompilerParams(
            collective_id=3, has_side_effects=True, vmem_limit_bytes=4 * 2**20
        ),
    )(mine)


def exchange_kernel(
    n, slots, kinds, idx_ref, vals_ref, code_ref, out_ref, code_out,
    packed, send_sem, recv_sem, csend_sem, crecv_sem, own_sem,
):
    me = lax.axis_index("aux")
    greet([lax.rem(me + d, n) for d in range(1, n)])

    turn = jnp.where(me < n // 2, n - 1, 1)

    def partner(step):
        return lax.rem(me + step * turn, n)

    def values(peer, count, sem):
        return pltpu.make_async_remote_copy(
            src_ref=packed.at[peer, pl.ds(0, count)],
            dst_ref=out_ref.at[me, pl.ds(0, count)],
            send_sem=send_sem.at[peer],
            recv_sem=recv_sem.at[sem],
            device_id={"aux": peer},
            device_id_type=MESH,
        )

    def codes(peer, sem):
        return pltpu.make_async_remote_copy(
            src_ref=code_ref.at[peer],
            dst_ref=code_out.at[me],
            send_sem=csend_sem.at[peer],
            recv_sem=crecv_sem.at[sem],
            device_id={"aux": peer},
            device_id_type=MESH,
        )

    def by_kind(device, act):
        if len(kinds) == 1:
            act(kinds[0])
            return
        kind = level(device, n)
        for number, count in enumerate(kinds):
            pl.when(kind == number)(functools.partial(act, count))

    def pack(peer):
        for k in range(slots):
            packed[peer, k] = vals_ref[idx_ref[peer * slots + k]]

    def send(d, carry):
        peer = partner(d)
        pack(peer)
        codes(peer, me).start()
        by_kind(peer, lambda count: values(peer, count, me).start())
        return carry

    lax.fori_loop(1, n, send, 0)
    pack(me)
    own_values = pltpu.make_async_copy(packed.at[me], out_ref.at[me], own_sem.at[0])
    own_codes = pltpu.make_async_copy(code_ref.at[me], code_out.at[me], own_sem.at[1])
    own_values.start()
    own_codes.start()
    own_values.wait()
    own_codes.wait()

    def finish(d, carry):
        peer = partner(d)
        codes(peer, peer).wait()
        by_kind(peer, lambda count: values(peer, count, me).wait_send())
        by_kind(me, lambda count: values(peer, count, peer).wait_recv())
        return carry

    lax.fori_loop(1, n, finish, 0)


def exchange(n, slots, kinds, number, idx, vals, codes):
    side = vals.shape[1]
    return pl.pallas_call(
        functools.partial(exchange_kernel, n, slots, kinds),
        out_shape=(
            jax.ShapeDtypeStruct((n, slots, side, side), vals.dtype),
            jax.ShapeDtypeStruct(codes.shape, codes.dtype),
        ),
        in_specs=[SMEM, VMEM, VMEM],
        out_specs=(ANY, ANY),
        scratch_shapes=[
            pltpu.VMEM((n, slots, side, side), vals.dtype),
            pltpu.SemaphoreType.DMA((n,)),
            pltpu.SemaphoreType.DMA((n,)),
            pltpu.SemaphoreType.DMA((n,)),
            pltpu.SemaphoreType.DMA((n,)),
            pltpu.SemaphoreType.DMA((2,)),
        ],
        compiler_params=pltpu.CompilerParams(
            collective_id=number, has_side_effects=True, vmem_limit_bytes=24 * 2**20
        ),
    )(idx, vals, codes)


def tile_kernel(
    n, slots, wide, code_ref, vals_hbm, coef_hbm, out_ref, vals_ref, coef_ref, acc, seen, sem
):
    side = vals_ref.shape[1]
    mid = MU // 2
    parts = coef_ref.shape[2] // wide

    def coef_copy(j):
        columns = pl.ds(j * wide, wide)
        return pltpu.make_async_copy(
            coef_hbm.at[:, :, columns], coef_ref.at[:, :, columns], sem.at[n + j]
        )

    def vals_copy(p):
        rows = pl.ds(p * slots, slots)
        return pltpu.make_async_copy(vals_hbm.at[rows], vals_ref.at[rows], sem.at[p])

    coef_copy(0).start()
    for p in range(n):
        vals_copy(p).start()
    for j in range(1, parts):
        coef_copy(j).start()

    def reset(key, carry):
        seen[key] = 0
        return carry

    lax.fori_loop(0, KEYS + 1, reset, 0)

    for j in range(parts):
        coef_copy(j).wait()
        columns = pl.ds(j * wide, wide)

        def add(step, carry):
            if j == 0:
                vals_copy(step).wait()
            for k in range(slots):
                s = step * slots + k
                code = code_ref[s]
                key = jnp.where(code >= 0, code % KEYS, KEYS)
                col = jnp.where(code >= 0, code // KEYS, 0)
                part = jnp.dot(
                    vals_ref[s], coef_ref[col, :, columns], preferred_element_type=jnp.float32
                )
                rows = pl.ds(pl.multiple_of(key % ROW_BLKS * side, side), side)
                begun = seen[key] == j + 1
                before = jnp.where(begun, acc[key // ROW_BLKS, rows, columns], 0.0)
                acc[key // ROW_BLKS, rows, columns] = before + part
                seen[key] = j + 1
            return carry

        lax.fori_loop(0, n, add, 0)

    out_ref[...] = jnp.zeros_like(out_ref)

    def against(left, right):
        return lax.dot_general(
            left, right, (((1,), (1,)), ((), ())), preferred_element_type=jnp.float32
        )

    def rounded(a):
        return jnp.concatenate(
            [
                jnp.where(
                    seen[a * ROW_BLKS + r] > 0, acc[a, r * side : (r + 1) * side, :], 0.0
                ).astype(jnp.bfloat16)
                for r in range(ROW_BLKS)
            ],
            axis=0,
        )

    def square(step, carry):
        h, g = rounded(2 * step), rounded(2 * step + 1)
        out_ref[:mid, :] += against(h[:mid], h) + against(g[:mid], g)
        out_ref[mid:, mid:] += against(h[mid:], h[mid:]) + against(g[mid:], g[mid:])
        return carry

    lax.fori_loop(0, AUX_DEV // 2, square, 0)
    out_ref[mid:, :mid] = out_ref[:mid, mid:].T


def tile(n, slots, codes, vals, coef):
    nocc = coef.shape[2]
    wide = nocc
    return pl.pallas_call(
        functools.partial(tile_kernel, n, slots, wide),
        out_shape=jax.ShapeDtypeStruct((MU, MU), jnp.float32),
        in_specs=[SMEM, ANY, ANY],
        out_specs=VMEM,
        scratch_shapes=[
            pltpu.VMEM(vals.shape, vals.dtype),
            pltpu.VMEM(coef.shape, coef.dtype),
            pltpu.VMEM((AUX_DEV + 1, MU, nocc), jnp.float32),
            pltpu.SMEM((KEYS + 1,), jnp.int32),
            pltpu.SemaphoreType.DMA((n + nocc // wide,)),
        ],
        compiler_params=pltpu.CompilerParams(vmem_limit_bytes=56 * 2**20),
    )(codes, vals, coef)


def reduce_kernel(
    n, scale, k_ref, out_ref, own, got1, sum1, got2, sum2, got3, send_sem, recv_sem, own_sem
):
    me = lax.axis_index("aux")
    far = n // 4
    c, y, z = me % 2, me // 2 % 2, me // 4
    pair, side = me + 1 - 2 * c, me + 2 - 4 * y
    order = list(range(far - 1, -1, -1))
    chunk = [paired(z, t, far) for t in range(far)]
    load = pltpu.make_async_copy(k_ref.at[:, :, c], own, own_sem)
    load.start()
    greet([pair, side] + [me + 4 * (chunk[t] - z) for t in range(1, far)])

    def copy(src, dst, sem, other):
        return pltpu.make_async_remote_copy(
            src_ref=src,
            dst_ref=dst,
            send_sem=send_sem.at[sem],
            recv_sem=recv_sem.at[sem],
            device_id={"aux": other},
            device_id_type=MESH,
        )

    def across(t, half, sem):
        spot = chunk[t]
        return copy(k_ref.at[spot, half, 1 - c], got1.at[spot, half], sem, pair)

    give = [across(t, 1 - y, t) for t in range(far)]
    keep = [across(t, y, far + t) for t in range(far)]
    beside = [copy(sum1.at[t], got2.at[t], 2 * far + t, side) for t in range(far)]
    along = [
        copy(sum2.at[t], got3.at[t], 3 * far + t, me + 4 * (chunk[t] - z)) for t in range(far)
    ]
    for t in order:
        give[t].start()
    for t in order:
        keep[t].start()
    load.wait()
    for t in order:
        give[t].wait()
        sum1[t] = own[chunk[t], 1 - y] + got1[chunk[t], 1 - y]
        beside[t].start()
    for t in order:
        keep[t].wait()
        mine = own[chunk[t], y] + got1[chunk[t], y]
        beside[t].wait()
        sum2[t] = mine + got2[t]
        if t:
            along[t].start()
    total = sum2[0]
    for t in order[:-1]:
        along[t].wait()
        total = total + got3[t]
    out_ref[...] = total * scale


def reduce_tile(n, scale, whole):
    far, rows = n // 4, MU // n
    f32 = jnp.float32
    return pl.pallas_call(
        functools.partial(reduce_kernel, n, scale),
        out_shape=jax.ShapeDtypeStruct((rows, MU), f32),
        in_specs=[ANY],
        out_specs=VMEM,
        scratch_shapes=[
            pltpu.VMEM((far, 2, rows, MU), f32),
            pltpu.VMEM((far, 2, rows, MU), f32),
            pltpu.VMEM((far, rows, MU), f32),
            pltpu.VMEM((far, rows, MU), f32),
            pltpu.VMEM((far, rows, MU), f32),
            pltpu.VMEM((far, rows, MU), f32),
            pltpu.SemaphoreType.DMA((4 * far,)),
            pltpu.SemaphoreType.DMA((4 * far,)),
            pltpu.SemaphoreType.DMA,
        ],
        compiler_params=pltpu.CompilerParams(
            collective_id=1, has_side_effects=True, vmem_limit_bytes=6 * 2**20
        ),
    )(whole.reshape(far, 2, 2, rows, MU))


def body(block_values, block_dest, block_aux, block_row, block_col, coefficients):
    n = lax.axis_size("aux")
    count, side = block_values.shape[:2]
    nocc = coefficients.shape[1]
    slots = 2 * count // n
    dest = block_dest[:, 0]
    tiered = slots >= 8
    if tiered:
        named = dest[:, None] == jnp.arange(128, dtype=jnp.int32)[None, :]
        mine = jnp.sum(named.astype(jnp.int32), axis=0)
        counts = gather_counts(n, jnp.broadcast_to(mine[None, :], (8, 128)))[:, 0, :n]
        most = jnp.max(counts, axis=0)
        score = (most * 4096 + jnp.sum(counts, axis=0)) * n - jnp.arange(n, dtype=jnp.int32)
        rank = jnp.sum((score[None, :] > score[:, None]).astype(jnp.int32), axis=1)
        lies, kinds = spread(n, slots)
        here = rank[:, None] == jnp.arange(n, dtype=jnp.int32)[None, :]
        device = jnp.sum(jnp.where(here, jnp.asarray(lies, jnp.int32)[None, :], 0), axis=1)
        kind = level(device, n)
        room = sum(jnp.where(kind == number, count, 0) for number, count in enumerate(kinds))
        fits = jnp.all(room >= most)
        dest = jnp.sum(jnp.where(named[:, :n], device[None, :], 0), axis=1)
    place = jnp.arange(count, dtype=jnp.int32)
    earlier = (dest[:, None] == dest[None, :]) & (place[:, None] > place[None, :])
    target = dest * slots + jnp.sum(earlier.astype(jnp.int32), axis=1)
    hit = target[None, :] == jnp.arange(n * slots, dtype=jnp.int32)[:, None]
    idx = jnp.sum(jnp.where(hit, place[None, :], 0), axis=1)
    code = block_col * KEYS + block_aux * ROW_BLKS + block_row
    sent = jnp.sum(jnp.where(hit, code[None, :] + 1, 0), axis=1) - 1
    sent = jnp.pad(sent.reshape(n, 1, slots), ((0, 0), (0, 7), (0, 128 - slots)))
    if tiered:
        values, codes = lax.cond(
            fits,
            functools.partial(exchange, n, slots, kinds, 0),
            functools.partial(exchange, n, slots, (slots,), 2),
            idx,
            block_values,
            sent,
        )
    else:
        values, codes = exchange(n, slots, (slots,), 2, idx, block_values, sent)
    whole = tile(
        n,
        slots,
        codes[:, 0, :slots].reshape(n * slots),
        values.reshape(n * slots, side, side),
        coefficients.reshape(-1, side, nocc),
    )
    return reduce_tile(n, 1.0 / nocc, whole)


def solution(mesh):
    placed = (
        P(("grp", "aux"), None, None),
        P(("grp", "aux"), None),
        P(("grp", "aux")),
        P(("grp", "aux")),
        P(("grp", "aux")),
        P("grp", None),
    )
    return jax.shard_map(
        body, mesh=mesh, in_specs=placed, out_specs=P(("grp", "aux"), None), check_vma=False
    )
```

```python
import functools

import jax
import jax.numpy as jnp
from jax import lax
from jax.experimental import pallas as pl
from jax.experimental.pallas import tpu as pltpu
from jax.sharding import PartitionSpec as P

ROW_BLKS = 4
AUX_DEV = 16
KEYS = ROW_BLKS * AUX_DEV
UNROLL = 8
MU = 512
MESH = pl.DeviceIdType.MESH
VMEM = pl.BlockSpec(memory_space=pltpu.VMEM)
SMEM = pl.BlockSpec(memory_space=pltpu.SMEM)
ANY = pl.BlockSpec(memory_space=pl.ANY)


def paired(me, d, n):
    peer, bit = 0, 1
    while bit < n:
        mine, other = me // bit % 2, d // bit % 2
        peer = peer + bit * (mine + other - 2 * mine * other)
        bit *= 2
    return peer


def greet(others):
    barrier = pltpu.get_barrier_semaphore()
    for other in others:
        pl.semaphore_signal(barrier, inc=1, device_id={"aux": other}, device_id_type=MESH)
    pl.semaphore_wait(barrier, len(others))


def level(device, n):
    chip = device // 2
    first = (chip < n // 8) | (chip >= n // 2 - n // 8)
    low = chip % 2 == 0
    upper = jnp.where(first, jnp.where(low, 0, 1), 2)
    return jnp.where(device % 2 == 0, upper, jnp.where(first & low, 4, 3))


def spread(n, slots):
    chips = range(n // 2)
    outer = [q for q in chips if q < n // 8 or q >= n // 2 - n // 8]
    order = [q for q in outer if q % 2 == 0] + [q for q in outer if q % 2]
    order += [q for q in chips if q not in outer]
    lies = [2 * q for q in order] + [2 * q + 1 for q in reversed(order)]
    return lies, tuple(-(-slots * eighths // 8) for eighths in (8, 7, 6, 5, 4))


def counts_kernel(n, mine_ref, all_ref, send_sem, recv_sem, own_sem):
    me = lax.axis_index("aux")
    greet([lax.rem(me + d, n) for d in range(1, n)])
    copies = [
        pltpu.make_async_remote_copy(
            src_ref=mine_ref,
            dst_ref=all_ref.at[me],
            send_sem=send_sem.at[d],
            recv_sem=recv_sem.at[d],
            device_id={"aux": lax.rem(me + d, n)},
            device_id_type=MESH,
        )
        for d in range(1, n)
    ]
    for one in copies:
        one.start()
    own = pltpu.make_async_copy(mine_ref, all_ref.at[me], own_sem)
    own.start()
    own.wait()
    for one in copies:
        one.wait()


def gather_counts(n, mine):
    return pl.pallas_call(
        functools.partial(counts_kernel, n),
        out_shape=jax.ShapeDtypeStruct((n,) + mine.shape, mine.dtype),
        in_specs=[VMEM],
        out_specs=VMEM,
        scratch_shapes=[
            pltpu.SemaphoreType.DMA((n,)),
            pltpu.SemaphoreType.DMA((n,)),
            pltpu.SemaphoreType.DMA,
        ],
        compiler_params=pltpu.CompilerParams(
            collective_id=3, has_side_effects=True, vmem_limit_bytes=4 * 2**20
        ),
    )(mine)


def exchange_kernel(
    n, slots, kinds, idx_ref, vals_ref, code_ref, out_ref, code_out,
    packed, send_sem, recv_sem, csend_sem, crecv_sem, own_sem,
):
    me = lax.axis_index("aux")
    greet([lax.rem(me + d, n) for d in range(1, n)])

    turn = jnp.where(me < n // 2, n - 1, 1)

    def partner(step):
        return lax.rem(me + step * turn, n)

    def values(peer, count, sem):
        return pltpu.make_async_remote_copy(
            src_ref=packed.at[peer, pl.ds(0, count)],
            dst_ref=out_ref.at[me, pl.ds(0, count)],
            send_sem=send_sem.at[peer],
            recv_sem=recv_sem.at[sem],
            device_id={"aux": peer},
            device_id_type=MESH,
        )

    def codes(peer, sem):
        return pltpu.make_async_remote_copy(
            src_ref=code_ref.at[peer],
            dst_ref=code_out.at[me],
            send_sem=csend_sem.at[peer],
            recv_sem=crecv_sem.at[sem],
            device_id={"aux": peer},
            device_id_type=MESH,
        )

    def by_kind(device, act):
        if len(kinds) == 1:
            act(kinds[0])
            return
        kind = level(device, n)
        for number, count in enumerate(kinds):
            pl.when(kind == number)(functools.partial(act, count))

    def pack(peer):
        for k in range(slots):
            packed[peer, k] = vals_ref[idx_ref[peer * slots + k]]

    def send(d, carry):
        peer = partner(d)
        pack(peer)
        codes(peer, me).start()
        by_kind(peer, lambda count: values(peer, count, me).start())
        return carry

    lax.fori_loop(1, n, send, 0)
    pack(me)
    own_values = pltpu.make_async_copy(packed.at[me], out_ref.at[me], own_sem.at[0])
    own_codes = pltpu.make_async_copy(code_ref.at[me], code_out.at[me], own_sem.at[1])
    own_values.start()
    own_codes.start()
    own_values.wait()
    own_codes.wait()

    def finish(d, carry):
        peer = partner(d)
        codes(peer, peer).wait()
        by_kind(peer, lambda count: values(peer, count, me).wait_send())
        by_kind(me, lambda count: values(peer, count, peer).wait_recv())
        return carry

    lax.fori_loop(1, n, finish, 0)


def exchange(n, slots, kinds, number, idx, vals, codes):
    side = vals.shape[1]
    return pl.pallas_call(
        functools.partial(exchange_kernel, n, slots, kinds),
        out_shape=(
            jax.ShapeDtypeStruct((n, slots, side, side), vals.dtype),
            jax.ShapeDtypeStruct(codes.shape, codes.dtype),
        ),
        in_specs=[SMEM, VMEM, VMEM],
        out_specs=(ANY, ANY),
        scratch_shapes=[
            pltpu.VMEM((n, slots, side, side), vals.dtype),
            pltpu.SemaphoreType.DMA((n,)),
            pltpu.SemaphoreType.DMA((n,)),
            pltpu.SemaphoreType.DMA((n,)),
            pltpu.SemaphoreType.DMA((n,)),
            pltpu.SemaphoreType.DMA((2,)),
        ],
        compiler_params=pltpu.CompilerParams(
            collective_id=number, has_side_effects=True, vmem_limit_bytes=24 * 2**20
        ),
    )(idx, vals, codes)


def tile_kernel(
    n, slots, code_ref, vals_hbm, coef_hbm, out_ref, vals_ref, coef_ref, acc, seen, listed, sem
):
    side = vals_ref.shape[1]
    mid = MU // 2
    vals_copy = pltpu.make_async_copy(vals_hbm, vals_ref, sem.at[0])
    coef_copy = pltpu.make_async_copy(coef_hbm, coef_ref, sem.at[1])
    vals_copy.start()
    coef_copy.start()

    def reset(key, carry):
        seen[key] = 0
        return carry

    lax.fori_loop(0, KEYS + 1, reset, 0)

    def note(s, count):
        listed[count] = s
        return count + jnp.where(code_ref[s] >= 0, 1, 0)

    count = lax.fori_loop(0, n * slots, note, jnp.int32(0))
    for k in range(UNROLL):
        listed[count + k] = 0
    vals_copy.wait()
    coef_copy.wait()

    def add(step, carry):
        for k in range(UNROLL):
            at = step * UNROLL + k
            s = listed[at]
            live = at < count
            code = code_ref[s]
            key = jnp.where(live, code % KEYS, KEYS)
            col = jnp.where(live, code // KEYS, 0)
            part = jnp.dot(vals_ref[s], coef_ref[col], preferred_element_type=jnp.float32)
            rows = pl.ds(pl.multiple_of(key % ROW_BLKS * side, side), side)
            before = jnp.where(seen[key] == 1, acc[key // ROW_BLKS, rows, :], 0.0)
            acc[key // ROW_BLKS, rows, :] = before + part
            seen[key] = 1
        return carry

    lax.fori_loop(0, (count + UNROLL - 1) // UNROLL, add, 0)
    out_ref[...] = jnp.zeros_like(out_ref)

    def against(left, right):
        return lax.dot_general(
            left, right, (((1,), (1,)), ((), ())), preferred_element_type=jnp.float32
        )

    def rounded(a):
        return jnp.concatenate(
            [
                jnp.where(
                    seen[a * ROW_BLKS + r] > 0, acc[a, r * side : (r + 1) * side, :], 0.0
                ).astype(jnp.bfloat16)
                for r in range(ROW_BLKS)
            ],
            axis=0,
        )

    def square(step, carry):
        h, g = rounded(2 * step), rounded(2 * step + 1)
        out_ref[:mid, :] += against(h[:mid], h) + against(g[:mid], g)
        out_ref[mid:, mid:] += against(h[mid:], h[mid:]) + against(g[mid:], g[mid:])
        return carry

    lax.fori_loop(0, AUX_DEV // 2, square, 0)
    out_ref[mid:, :mid] = out_ref[:mid, mid:].T


def tile(n, slots, codes, vals, coef):
    nocc = coef.shape[2]
    return pl.pallas_call(
        functools.partial(tile_kernel, n, slots),
        out_shape=jax.ShapeDtypeStruct((MU, MU), jnp.float32),
        in_specs=[SMEM, ANY, ANY],
        out_specs=VMEM,
        scratch_shapes=[
            pltpu.VMEM(vals.shape, vals.dtype),
            pltpu.VMEM(coef.shape, coef.dtype),
            pltpu.VMEM((AUX_DEV + 1, MU, nocc), jnp.float32),
            pltpu.SMEM((KEYS + 1,), jnp.int32),
            pltpu.SMEM((n * slots + UNROLL,), jnp.int32),
            pltpu.SemaphoreType.DMA((2,)),
        ],
        compiler_params=pltpu.CompilerParams(vmem_limit_bytes=56 * 2**20),
    )(codes, vals, coef)


def reduce_kernel(
    n, scale, k_ref, out_ref, own, got1, sum1, got2, sum2, got3, send_sem, recv_sem, own_sem
):
    me = lax.axis_index("aux")
    far = n // 4
    c, y, z = me % 2, me // 2 % 2, me // 4
    pair, side = me + 1 - 2 * c, me + 2 - 4 * y
    order = list(range(far - 1, -1, -1))
    chunk = [paired(z, t, far) for t in range(far)]
    load = pltpu.make_async_copy(k_ref.at[:, :, c], own, own_sem)
    load.start()
    greet([pair, side] + [me + 4 * (chunk[t] - z) for t in range(1, far)])

    def copy(src, dst, sem, other):
        return pltpu.make_async_remote_copy(
            src_ref=src,
            dst_ref=dst,
            send_sem=send_sem.at[sem],
            recv_sem=recv_sem.at[sem],
            device_id={"aux": other},
            device_id_type=MESH,
        )

    def across(t, half, sem):
        spot = chunk[t]
        return copy(k_ref.at[spot, half, 1 - c], got1.at[spot, half], sem, pair)

    give = [across(t, 1 - y, t) for t in range(far)]
    keep = [across(t, y, far + t) for t in range(far)]
    beside = [copy(sum1.at[t], got2.at[t], 2 * far + t, side) for t in range(far)]
    along = [
        copy(sum2.at[t], got3.at[t], 3 * far + t, me + 4 * (chunk[t] - z)) for t in range(far)
    ]
    for t in order:
        give[t].start()
    for t in order:
        keep[t].start()
    load.wait()
    for t in order:
        give[t].wait()
        sum1[t] = own[chunk[t], 1 - y] + got1[chunk[t], 1 - y]
        beside[t].start()
    for t in order:
        keep[t].wait()
        mine = own[chunk[t], y] + got1[chunk[t], y]
        beside[t].wait()
        sum2[t] = mine + got2[t]
        if t:
            along[t].start()
    total = sum2[0]
    for t in order[:-1]:
        along[t].wait()
        total = total + got3[t]
    out_ref[...] = total * scale


def reduce_tile(n, scale, whole):
    far, rows = n // 4, MU // n
    f32 = jnp.float32
    return pl.pallas_call(
        functools.partial(reduce_kernel, n, scale),
        out_shape=jax.ShapeDtypeStruct((rows, MU), f32),
        in_specs=[ANY],
        out_specs=VMEM,
        scratch_shapes=[
            pltpu.VMEM((far, 2, rows, MU), f32),
            pltpu.VMEM((far, 2, rows, MU), f32),
            pltpu.VMEM((far, rows, MU), f32),
            pltpu.VMEM((far, rows, MU), f32),
            pltpu.VMEM((far, rows, MU), f32),
            pltpu.VMEM((far, rows, MU), f32),
            pltpu.SemaphoreType.DMA((4 * far,)),
            pltpu.SemaphoreType.DMA((4 * far,)),
            pltpu.SemaphoreType.DMA,
        ],
        compiler_params=pltpu.CompilerParams(
            collective_id=1, has_side_effects=True, vmem_limit_bytes=56 * 2**20
        ),
    )(whole.reshape(far, 2, 2, rows, MU))


def body(block_values, block_dest, block_aux, block_row, block_col, coefficients):
    n = lax.axis_size("aux")
    count, side = block_values.shape[:2]
    nocc = coefficients.shape[1]
    slots = 2 * count // n
    dest = block_dest[:, 0]
    tiered = slots >= 8
    if tiered:
        named = dest[:, None] == jnp.arange(128, dtype=jnp.int32)[None, :]
        mine = jnp.sum(named.astype(jnp.int32), axis=0)
        counts = gather_counts(n, jnp.broadcast_to(mine[None, :], (8, 128)))[:, 0, :n]
        most = jnp.max(counts, axis=0)
        score = (most * 4096 + jnp.sum(counts, axis=0)) * n - jnp.arange(n, dtype=jnp.int32)
        rank = jnp.sum((score[None, :] > score[:, None]).astype(jnp.int32), axis=1)
        lies, kinds = spread(n, slots)
        here = rank[:, None] == jnp.arange(n, dtype=jnp.int32)[None, :]
        device = jnp.sum(jnp.where(here, jnp.asarray(lies, jnp.int32)[None, :], 0), axis=1)
        kind = level(device, n)
        room = sum(jnp.where(kind == number, count, 0) for number, count in enumerate(kinds))
        fits = jnp.all(room >= most)
        dest = jnp.sum(jnp.where(named[:, :n], device[None, :], 0), axis=1)
    place = jnp.arange(count, dtype=jnp.int32)
    earlier = (dest[:, None] == dest[None, :]) & (place[:, None] > place[None, :])
    target = dest * slots + jnp.sum(earlier.astype(jnp.int32), axis=1)
    hit = target[None, :] == jnp.arange(n * slots, dtype=jnp.int32)[:, None]
    idx = jnp.sum(jnp.where(hit, place[None, :], 0), axis=1)
    code = block_col * KEYS + block_aux * ROW_BLKS + block_row
    sent = jnp.sum(jnp.where(hit, code[None, :] + 1, 0), axis=1) - 1
    sent = jnp.pad(sent.reshape(n, 1, slots), ((0, 0), (0, 7), (0, 128 - slots)))
    if tiered:
        values, codes = lax.cond(
            fits,
            functools.partial(exchange, n, slots, kinds, 0),
            functools.partial(exchange, n, slots, (slots,), 2),
            idx,
            block_values,
            sent,
        )
    else:
        values, codes = exchange(n, slots, (slots,), 2, idx, block_values, sent)
    whole = tile(
        n,
        slots,
        codes[:, 0, :slots].reshape(n * slots),
        values.reshape(n * slots, side, side),
        coefficients.reshape(-1, side, nocc),
    )
    return reduce_tile(n, 1.0 / nocc, whole)


def solution(mesh):
    placed = (
        P(("grp", "aux"), None, None),
        P(("grp", "aux"), None),
        P(("grp", "aux")),
        P(("grp", "aux")),
        P(("grp", "aux")),
        P("grp", None),
    )
    return jax.shard_map(
        body, mesh=mesh, in_specs=placed, out_specs=P(("grp", "aux"), None), check_vma=False
    )
```
